32 devices in a mesh: dp: 16 (over z, x, core), tensor: 2 (over y).
Axes of the slice: x: 2, y: 2, z: 4, core: 2. Of those that a mesh axis runs over, the one named last changes fastest.
Arguments:
- inputs: bfloat16 [8192, 2048], P('dp', 'tensor'), may hold values from -6 to 6
- out_grad: bfloat16 [8192, 2048], P('dp', 'tensor'), may hold values from -6 to 6
- lengths: int32 [16], replicated, may hold values from 128 to 512, as said below
- dealing: int32 [16], replicated, may hold values from 0 to 15, each once
- qkv_weight: bfloat16 [3, 2048, 2048], P(None, 'dp', 'tensor'), may hold values from -0.125 to 0.125
- qv_bias: bfloat16 [2, 32, 64], P(None, 'tensor', 'dp'), may hold values from -0.29882812 to 0.29882812
- out_weight: bfloat16 [2048, 2048], P('tensor', 'dp'), may hold values from -2 to 2
- out_bias: bfloat16 [2048], P('dp'), may hold values from -1.796875 to 1.796875
- attn_gain: bfloat16 [2048], P('dp'), may hold values from 0.099609375 to 1.8984375
- attn_shift: bfloat16 [2048], P('dp'), may hold values from -1.796875 to 1.796875
- up_weight: bfloat16 [2048, 8192], P('dp', 'tensor'), may hold values from -0.125 to 0.125
- up_bias: bfloat16 [128, 64], P('tensor', 'dp'), may hold values from -3 to 3
- down_weight: bfloat16 [8192, 2048], P('tensor', 'dp'), may hold values from -0.0625 to 0.0625
- down_bias: bfloat16 [2048], P('dp'), may hold values from -1.796875 to 1.796875
- ffn_gain: bfloat16 [2048], P('dp'), may hold values from 0.099609375 to 1.8984375
- ffn_shift: bfloat16 [2048], P('dp'), may hold values from -1.796875 to 1.796875
Outputs:
- outputs: bfloat16 [8192, 2048], P('dp', 'tensor')
- in_grad: bfloat16 [8192, 2048], P('dp', 'tensor')
- qkv_grad: float32 [3, 2048, 2048], P(None, 'dp', 'tensor')
- qv_bias_grad: float32 [2, 32, 64], P(None, 'tensor', 'dp')
- out_weight_grad: float32 [2048, 2048], P('tensor', 'dp')
- out_bias_grad: float32 [2048], P('dp')
- attn_gain_grad: float32 [2048], P('dp')
- attn_shift_grad: float32 [2048], P('dp')
- up_weight_grad: float32 [2048, 8192], P('dp', 'tensor')
- up_bias_grad: float32 [128, 64], P('tensor', 'dp')
- down_weight_grad: float32 [8192, 2048], P('tensor', 'dp')
- down_bias_grad: float32 [2048], P('dp')
- ffn_gain_grad: float32 [2048], P('dp')
- ffn_shift_grad: float32 [2048], P('dp')
The draws below stay inside these ranges and needn't reach their ends.
Inputs may be any that keep to these rules, and one draw needn't show every extreme that they name: `lengths`: the longest sequence has exactly 512 tokens. `dealing`: each sequence appears once.
All inputs are finite; a program needn't handle non-finite values.
Results may differ from the reference program's by a relative error of at most 0.02.
Values may be sent and summed in bfloat16 or wider, within the bound.
No kernel may reach another device: no remote copies, remote signals or barrier semaphores. Data moves between devices by JAX's collectives and lax.ppermute only.
A program may use at most 320 MiB of HBM per device.

```python
import math
import jax
import jax.numpy as jnp
from jax import lax

D = 2048
H = 16
HD = 128
FF = 8192
TOK_GRP = 512
SEQS = 16
TOKENS = 8192


def draw_lengths(key, part):
    key = jax.random.fold_in(key, 11)
    length_key, place_key = jax.random.split(key)
    drawn = jax.random.randint(length_key, (SEQS,), TOK_GRP // 4, TOK_GRP + 1)
    longest_at = jax.random.randint(place_key, (), 0, SEQS)
    return jnp.where(jnp.arange(SEQS) == longest_at, TOK_GRP, drawn).astype(jnp.int32)


def shard_levels(rng, extent, shards, low, largest):
    level = 1.0
    for axis_at, parts in shards:
        steps = jax.random.uniform(jax.random.fold_in(jax.random.fold_in(rng, 6), axis_at), (parts,), jnp.float32, low / len(shards), largest / len(shards))
        level = level * jnp.repeat(jnp.exp(steps), extent[axis_at] // parts).reshape((-1,) + (1,) * (len(extent) - 1 - axis_at))
    return level


def normal_values(stream_key, dims, scale, bound, cuts=(), kind=jnp.bfloat16):
    level = shard_levels(stream_key, dims, cuts, -0.22, 0.18) if cuts else 1.0
    values = jax.random.normal(stream_key, dims, jnp.float32) * scale * level
    return jnp.minimum(jnp.maximum(values, -bound), bound).astype(kind)


def setup_inputs(seed: int = 0) -> dict:
    streams_of = jax.random.split(jax.random.key(seed), 17)
    inputs = normal_values(streams_of[0], (TOKENS, D), 1.0, 6.0, ((0, 16), (1, 2)))
    out_grad = normal_values(streams_of[1], (TOKENS, D), 1.0, 6.0, ((0, 16), (1, 2)))
    lengths = draw_lengths(jax.random.fold_in(streams_of[16], 71), 0)
    dealing = jax.random.permutation(streams_of[3], SEQS).astype(jnp.int32)
    qkv_weight = normal_values(streams_of[4], (3, D, D), D ** -0.5, 0.125, ((1, 16), (2, 2)))
    qv_bias = normal_values(streams_of[5], (2, D // 64, 64), 0.05, 0.29882812, ((1, 2), (2, 16)))
    out_weight = normal_values(streams_of[6], (D, D), (max(1, D * 2 // TOK_GRP)) ** -0.5, 2.0, ((0, 2), (1, 16)))
    out_bias = normal_values(streams_of[7], (D,), 0.3, 1.796875, ((0, 16),))
    attn_gain = jnp.clip(1.0 + 0.18 * jax.random.normal(streams_of[8], (D,), jnp.float32), 0.099609375, 1.8984375).astype(jnp.bfloat16)
    attn_shift = normal_values(streams_of[9], (D,), 0.3, 1.796875, ((0, 16),))
    up_weight = normal_values(streams_of[10], (D, FF), D ** -0.5, 0.125, ((0, 16), (1, 2)))
    up_bias = normal_values(streams_of[11], (FF // 64, 64), 0.5, 3.0, ((0, 2), (1, 16)))
    down_weight = normal_values(streams_of[12], (FF, D), FF ** -0.5, 0.0625, ((0, 2), (1, 16)))
    down_bias = normal_values(streams_of[13], (D,), 0.3, 1.796875, ((0, 16),))
    ffn_gain = jnp.clip(1.0 + 0.18 * jax.random.normal(streams_of[14], (D,), jnp.float32), 0.099609375, 1.8984375).astype(jnp.bfloat16)
    ffn_shift = normal_values(streams_of[15], (D,), 0.3, 1.796875, ((0, 16),))
    return {"inputs": inputs, "out_grad": out_grad, "lengths": lengths, "dealing": dealing, "qkv_weight": qkv_weight, "qv_bias": qv_bias, "out_weight": out_weight, "out_bias": out_bias, "attn_gain": attn_gain, "attn_shift": attn_shift, "up_weight": up_weight, "up_bias": up_bias, "down_weight": down_weight, "down_bias": down_bias, "ffn_gain": ffn_gain, "ffn_shift": ffn_shift}


@jax.custom_vjp
def low(v):
    return lax.optimization_barrier(v.astype(jnp.bfloat16)).astype(jnp.float32)

@jax.custom_vjp
def low_back(v):
    return v

def low_keep(v):
    return (low(v), None)

def low_pass(kept, grad):
    return (grad,)

def back_keep(v):
    return (v, None)

def back_low(kept, grad):
    return (low(grad),)
low.defvjp(low_keep, low_pass)
low_back.defvjp(back_keep, back_low)
highest = lax.Precision.HIGHEST
epsilon = 1e-05
neg_large = -1e+30

def layer_norm(hidden, gain, shift):
    center = hidden - lax.optimization_barrier(jnp.mean(hidden, axis=-1, keepdims=True))
    spread = lax.optimization_barrier(jnp.mean(center * center, axis=-1, keepdims=True))
    return center * lax.rsqrt(spread + epsilon) * gain + shift

def layer_block(rows, valid_keys, params):
    qkv_w, qv_b, out_w, out_b, gain_one, shift_one, up_w, up_b, down_w, down_b, gain_two, shift_two = params
    batch = rows.shape[0]
    projected = jnp.einsum('gld,cde->cgle', rows, qkv_w, precision=highest)
    queries = low_back(low(projected[0] + qv_b[0]))
    key_rows = low_back(low(projected[1]))
    value_rows = low_back(low(projected[2] + qv_b[1]))
    head_shape = (batch, TOK_GRP, H, HD)
    scores = jnp.einsum('gqhe,gkhe->ghqk', queries.reshape(head_shape), key_rows.reshape(head_shape), precision=highest) * HD ** (-0.5)
    scores = low_back(jnp.where(valid_keys[:, None, None, :], scores, neg_large))
    top = lax.optimization_barrier(jnp.max(scores, axis=-1, keepdims=True))
    expo = jnp.exp(scores - top)
    probs = low(expo / lax.optimization_barrier(jnp.sum(expo, axis=-1, keepdims=True)))
    context = jnp.einsum('ghqk,gkhe->gqhe', probs, value_rows.reshape(head_shape), precision=highest)
    context = low_back(low(context.reshape(batch, TOK_GRP, D)))
    attended = low_back(jnp.einsum('gle,ed->gld', context, out_w, precision=highest) + out_b)
    first = layer_norm(rows + attended, gain_one, shift_one)
    pre_act = low_back(jnp.einsum('gld,df->glf', low(first), up_w, precision=highest) + up_b)
    hidden = low(jax.nn.gelu(pre_act, approximate=True))
    mixed = low_back(jnp.einsum('glf,fd->gld', hidden, down_w, precision=highest) + down_b)
    return layer_norm(first + mixed, gain_two, shift_two)

def reference(inputs, out_grad, lengths, dealing, qkv_weight, qv_bias, out_weight, out_bias, attn_gain, attn_shift, up_weight, up_bias, down_weight, down_bias, ffn_gain, ffn_shift):
    per_peer = TOK_GRP // SEQS
    batch = math.gcd(SEQS, max(1, 4096 // TOK_GRP))
    order = dealing.astype(jnp.int32)
    dealt_lengths = jnp.take(lengths.astype(jnp.int32), order)
    valid_keys = jnp.arange(TOK_GRP, dtype=jnp.int32)[None, :] < dealt_lengths[:, None]
    params = (qkv_weight, qv_bias.reshape(2, D), out_weight, out_bias, attn_gain, attn_shift, up_weight, up_bias.reshape(FF), down_weight, down_bias, ffn_gain, ffn_shift)
    params = tuple((member.astype(jnp.float32) for member in params))

    def forward(flat, weights):
        seqs = flat.reshape(SEQS, SEQS, per_peer, D).transpose(1, 2, 0, 3).reshape(SEQS, TOK_GRP, D)
        seqs = jnp.take(seqs, order, axis=0)
        step = jax.checkpoint(lambda pair: layer_block(pair[0], pair[1], weights))
        result = lax.map(step, (seqs.reshape(SEQS // batch, batch, TOK_GRP, D), valid_keys.reshape(SEQS // batch, batch, TOK_GRP)))
        return result.reshape(SEQS * TOK_GRP, D)
    outputs, pull = jax.vjp(forward, inputs.astype(jnp.float32), params)
    in_grad, grads = pull(out_grad.astype(jnp.float32))
    return (outputs.astype(jnp.bfloat16), in_grad.astype(jnp.bfloat16), grads[0], grads[1].reshape(2, D // 64, 64), grads[2], grads[3], grads[4], grads[5], grads[6], grads[7].reshape(FF // 64, 64), grads[8], grads[9], grads[10], grads[11])
```

```python
import jax
import jax.numpy as jnp
from jax import lax
from jax.sharding import PartitionSpec as P

HD = 128


epsilon = 1e-05
neg_large = -1e30
low = jnp.bfloat16
wide = jnp.float32


def gelu_value(values):
    return jax.nn.gelu(values, approximate=True)


def norm_forward(hidden, gain, shift):
    center = hidden - jnp.mean(hidden, axis=-1, keepdims=True)
    inverse = lax.rsqrt(jnp.mean(center * center, axis=-1, keepdims=True) + epsilon)
    normed = center * inverse
    return (normed * gain + shift, normed, inverse)


def norm_backward(grad_rows, normed, inverse, gain):
    scaled = grad_rows * gain
    mean_first = jnp.mean(scaled, axis=-1, keepdims=True)
    mean_second = jnp.mean(scaled * normed, axis=-1, keepdims=True)
    result = inverse * (scaled - mean_first - normed * mean_second)
    return (result, jnp.sum(grad_rows * normed, axis=0), jnp.sum(grad_rows, axis=0))


def dot(left, right):
    return jnp.dot(left, right, preferred_element_type=wide)


def dot_ta(left, right):
    return jnp.einsum("la,lb->ab", left, right, preferred_element_type=wide)


def dot_tb(left, right):
    return jnp.einsum("la,ba->lb", left, right, preferred_element_type=wide)


def take(array, start, size, axis):
    return lax.dynamic_slice_in_dim(array, start, size, axis)


def local(
    inputs,
    out_grad,
    lengths,
    dealing,
    qkv_weight,
    qv_bias,
    out_weight,
    out_bias,
    attn_gain,
    attn_shift,
    up_weight,
    up_bias,
    down_weight,
    down_bias,
    ffn_gain,
    ffn_shift,
):
    groups = lax.axis_size("dp")
    ring_size = groups // 4
    index = lax.axis_index("dp")
    core, side, ring = index % 2, (index // 2) % 2, index // 4
    lane = lax.axis_index("tensor")
    core_pairs = [(i, i ^ 1) for i in range(groups)]
    side_pairs = [(i, i ^ 2) for i in range(groups)]
    ring_pairs = [(i, (i + 4) % groups) for i in range(groups)]

    def core_swap(array):
        return lax.ppermute(array, "dp", core_pairs)

    def side_swap(array):
        return lax.ppermute(array, "dp", side_pairs)

    def ring_shift(array):
        return lax.ppermute(array, "dp", ring_pairs)

    def lane_swap(array):
        return lax.ppermute(array, "tensor", [(0, 1), (1, 0)])

    def in_order(bit, mine, theirs, axis):
        first = jnp.where(bit == 0, mine, theirs)
        second = jnp.where(bit == 0, theirs, mine)
        return jnp.concatenate([first, second], axis=axis)

    seq_len, half = inputs.shape
    width = 2 * half
    per_peer = seq_len // groups
    shard = width // groups
    block = width // ring_size
    half_block = block // 2
    token_half = seq_len // 2

    small = jnp.concatenate(
        [
            v.reshape(-1)
            for v in (
                qv_bias,
                up_bias,
                out_bias,
                attn_gain,
                attn_shift,
                down_bias,
                ffn_gain,
                ffn_shift,
            )
        ]
    )
    small_all = lax.all_gather(small, "dp", axis=0, tiled=False)
    cut_one = qv_bias.size
    cut_two = cut_one + up_bias.size
    qv_full = (
        small_all[:, :cut_one]
        .reshape((groups,) + qv_bias.shape)
        .transpose(1, 2, 0, 3)
        .reshape(2, half)
    )
    up_bias_full = (
        small_all[:, cut_one:cut_two]
        .reshape((groups,) + up_bias.shape)
        .transpose(1, 0, 2)
        .reshape(-1)
    )
    vectors = (
        small_all[:, cut_two:].reshape(groups, 6, shard).transpose(1, 0, 2).reshape(6, width)
    ).astype(wide)
    out_bias_full, gain_one, shift_one, down_bias_full, gain_two, shift_two = vectors
    quarter = half // 2
    qv_rows = take(qv_full, core * quarter, quarter, 1)
    unit_half = up_bias_full.shape[0] // 2
    up_bias_mine = take(up_bias_full, core * unit_half, unit_half, 0)

    local_rows = inputs.reshape(groups, per_peer, half).swapaxes(0, 1)
    sending = jnp.take(local_rows, dealing, axis=1)
    arrived = lax.all_to_all(sending, "dp", split_axis=1, concat_axis=1, tiled=True)
    tokens = arrived.reshape(seq_len, half)
    own_rows = in_order(lane, tokens, lane_swap(tokens), 1)
    all_rows = in_order(core, own_rows, core_swap(own_rows), 0)
    residual = take(own_rows, lane * token_half, token_half, 0)
    grad_keep = take(out_grad, lane * token_half, token_half, 0)
    grad_send = take(out_grad, (1 - lane) * token_half, token_half, 0)
    cotangent = in_order(lane, grad_keep, lane_swap(grad_send), 1)

    def core_split(weight, unit_axis, width_axis):
        size = weight.shape[unit_axis] // 2
        mine = take(weight, core * size, size, unit_axis)
        sent = take(weight, (1 - core) * size, size, unit_axis)
        return in_order(core, mine, core_swap(sent), width_axis)

    def gather(piece):
        pieces = []
        for step in range(ring_size):
            if step:
                piece = ring_shift(piece)
            pieces.append((piece, side_swap(piece)))
        return pieces

    def assemble(pieces, axis):
        shape = list(pieces[0][0].shape)
        shape[axis] = width
        full = jnp.zeros(shape, low)
        for step, (mine, theirs) in enumerate(pieces):
            place = ((ring - step) % ring_size) * 2
            full = lax.dynamic_update_slice_in_dim(
                full, mine, (place + side) * half_block, axis
            )
            full = lax.dynamic_update_slice_in_dim(
                full, theirs, (place + 1 - side) * half_block, axis
            )
        return full

    qkv_full = assemble(gather(core_split(qkv_weight, 2, 1)), 1)
    out_full = assemble(gather(core_split(out_weight, 0, 1)), 1)
    up_full = assemble(gather(core_split(up_weight, 1, 0)), 0)
    down_full = assemble(gather(core_split(down_weight, 0, 1)), 1)

    def group_sum(partial):
        keep = take(partial, core * seq_len, seq_len, 0)
        sent = take(partial, (1 - core) * seq_len, seq_len, 0).astype(low)
        summed = keep + core_swap(sent).astype(wide)
        keep = take(summed, lane * token_half, token_half, 0)
        sent = take(summed, (1 - lane) * token_half, token_half, 0).astype(low)
        return keep + lane_swap(sent).astype(wide)

    def group_gather(rows):
        own = in_order(lane, rows, lane_swap(rows), 0)
        return own, in_order(core, own, core_swap(own), 0)

    heads = quarter // HD
    scale = HD ** (-0.5)
    rows = 2 * seq_len
    projected = jnp.einsum("ld,cde->cle", all_rows, qkv_full, preferred_element_type=wide)
    split = (2, seq_len, heads, HD)
    query = (projected[0] + qv_rows[0]).astype(low).reshape(split)
    key = projected[1].astype(low).reshape(split)
    value = (projected[2] + qv_rows[1]).astype(low).reshape(split)
    pair_lengths = jnp.take(lengths, take(dealing, (index // 2) * 2, 2, 0))
    valid = jnp.arange(seq_len, dtype=jnp.int32)[None, :] < pair_lengths[:, None]
    scores = (
        jnp.einsum("sqhe,skhe->shqk", query, key, preferred_element_type=wide) * scale
    )
    scores = jnp.where(valid[:, None, None, :], scores, neg_large)
    top = jnp.max(scores, axis=-1, keepdims=True)
    expo = jnp.exp(scores - top)
    probs = expo / jnp.sum(expo, axis=-1, keepdims=True)
    probs_low = probs.astype(low)
    context = (
        jnp.einsum("shqk,skhe->sqhe", probs_low, value, preferred_element_type=wide)
        .astype(low)
        .reshape(rows, quarter)
    )
    attended = group_sum(dot(context, out_full)) + out_bias_full
    first, normed_one, inverse_one = norm_forward(
        residual.astype(wide) + attended, gain_one, shift_one
    )
    unused, first_low = group_gather(first.astype(low))

    pre_act = dot(first_low, up_full) + up_bias_mine
    hidden = gelu_value(pre_act).astype(low)
    mixed = group_sum(dot(hidden, down_full)) + down_bias_full
    final, normed_two, inverse_two = norm_forward(first + mixed, gain_two, shift_two)
    final_low = final.astype(low)
    out_keep = take(final_low, lane * half, half, 1)
    out_send = take(final_low, (1 - lane) * half, half, 1)
    outputs = in_order(lane, out_keep, lane_swap(out_send), 0)

    second_grad, gain_two_grad, shift_two_grad = norm_backward(
        cotangent.astype(wide), normed_two, inverse_two, gain_two
    )
    mixed_low = second_grad.astype(low)
    down_bias_grad = jnp.sum(mixed_low, axis=0, dtype=wide)
    unused, mixed_grad = group_gather(mixed_low)

    def reduce(make, width_axis, unit_axis):
        total = None
        for step in range(ring_size):
            place = ((ring - 1 - step) % ring_size) * block
            partial = make(place)
            keep = take(partial, side * half_block, half_block, width_axis)
            sent = take(partial, (1 - side) * half_block, half_block, width_axis)
            both = keep + side_swap(sent.astype(low)).astype(wide)
            total = both if total is None else both + ring_shift(total.astype(low)).astype(wide)
        keep = take(total, core * shard, shard, width_axis)
        sent = take(total, (1 - core) * shard, shard, width_axis)
        return in_order(core, keep, core_swap(sent.astype(low)).astype(wide), unit_axis)

    down_weight_grad = reduce(
        lambda place: dot_ta(hidden, take(mixed_grad, place, block, 1)), 1, 0
    )
    hidden_grad = dot_tb(mixed_grad, down_full)
    unused_value, gelu_pull = jax.vjp(gelu_value, pre_act)
    pre_grad = gelu_pull(hidden_grad)[0].astype(low)
    up_bias_grad = jnp.sum(pre_grad, axis=0, dtype=wide)
    up_weight_grad = reduce(
        lambda place: dot_ta(take(first_low, place, block, 1), pre_grad), 0, 1
    )
    first_grad = second_grad + group_sum(dot_tb(pre_grad, up_full))
    attn_total_grad, gain_one_grad, shift_one_grad = norm_backward(
        first_grad, normed_one, inverse_one, gain_one
    )
    attended_low = attn_total_grad.astype(low)
    out_bias_grad = jnp.sum(attended_low, axis=0, dtype=wide)
    own_attended, attended_grad = group_gather(attended_low)
    out_weight_grad = reduce(
        lambda place: dot_ta(context, take(attended_grad, place, block, 1)), 1, 0
    )
    context_grad = dot_tb(attended_grad, out_full).astype(low).reshape(split)

    prob_grad = jnp.einsum("sqhe,skhe->shqk", context_grad, value, preferred_element_type=wide)
    score_grad = (
        probs * (prob_grad - jnp.sum(prob_grad * probs, axis=-1, keepdims=True))
    ).astype(low)
    query_grad = (
        jnp.einsum("shqk,skhe->sqhe", score_grad, key, preferred_element_type=wide) * scale
    )
    key_grad = (
        jnp.einsum("shqk,sqhe->skhe", score_grad, query, preferred_element_type=wide) * scale
    )
    value_grad = jnp.einsum(
        "shqk,sqhe->skhe", probs_low, context_grad, preferred_element_type=wide
    )
    stacked = jnp.stack(
        [g.astype(low).reshape(rows, quarter) for g in (query_grad, key_grad, value_grad)]
    )
    qv_grad = jnp.sum(stacked[0::2], axis=1, dtype=wide)
    qkv_grad = reduce(
        lambda place: jnp.einsum(
            "ld,cle->cde", take(all_rows, place, block, 1), stacked, preferred_element_type=wide
        ),
        1,
        2,
    )
    part_grad = jnp.einsum("cle,cde->ld", stacked, qkv_full, preferred_element_type=wide)
    keep = take(part_grad, core * seq_len, seq_len, 0)
    sent = take(part_grad, (1 - core) * seq_len, seq_len, 0).astype(low)
    own_part = keep + core_swap(sent).astype(wide)
    keep = take(own_part, lane * half, half, 1) + take(own_attended, lane * half, half, 1).astype(
        wide
    )
    sent = take(own_part, (1 - lane) * half, half, 1).astype(low)
    in_half = (keep + lane_swap(sent).astype(wide)).astype(low)
    back_rows = in_half.reshape(per_peer, groups, half)
    returned = lax.all_to_all(back_rows, "dp", split_axis=1, concat_axis=1, tiled=True)
    inverse_order = (
        jnp.zeros((groups,), jnp.int32).at[dealing].set(jnp.arange(groups, dtype=jnp.int32))
    )
    in_grad = jnp.take(returned, inverse_order, axis=1).swapaxes(0, 1).reshape(seq_len, half)

    def spread(mine, size):
        full = jnp.zeros(mine.shape[:-1] + (2 * size,), wide)
        return lax.dynamic_update_slice_in_dim(full, mine, core * size, mine.ndim - 1)

    qv_spread = (
        spread(qv_grad, quarter)
        .reshape(2, qv_bias.shape[1], groups, qv_bias.shape[2])
        .transpose(2, 0, 1, 3)
        .reshape(groups, -1)
    )
    up_spread = (
        spread(up_bias_grad, unit_half)
        .reshape(up_bias.shape[0], groups, up_bias.shape[1])
        .transpose(1, 0, 2)
        .reshape(groups, -1)
    )
    vector_spread = (
        jnp.stack(
            [
                out_bias_grad,
                gain_one_grad,
                shift_one_grad,
                down_bias_grad,
                gain_two_grad,
                shift_two_grad,
            ]
        )
        .reshape(6, groups, shard)
        .transpose(1, 0, 2)
        .reshape(groups, -1)
    )
    packed = jnp.concatenate([qv_spread, up_spread, vector_spread], axis=1)
    exchanged = lax.all_to_all(packed, "dp", split_axis=0, concat_axis=0, tiled=True)
    small_sum = jnp.sum(exchanged, axis=0)
    vector_sum = small_sum[cut_two:]
    vector_sum = (vector_sum + lane_swap(vector_sum)).reshape(6, shard)
    return (
        outputs,
        in_grad,
        qkv_grad,
        small_sum[:cut_one].reshape(qv_bias.shape),
        out_weight_grad,
        vector_sum[0],
        vector_sum[1],
        vector_sum[2],
        up_weight_grad,
        small_sum[cut_one:cut_two].reshape(up_bias.shape),
        down_weight_grad,
        vector_sum[3],
        vector_sum[4],
        vector_sum[5],
    )


def solution(mesh):
    placed = (
        P("dp", "tensor"),
        P("dp", "tensor"),
        P(),
        P(),
        P(None, "dp", "tensor"),
        P(None, "tensor", "dp"),
        P("tensor", "dp"),
        P("dp"),
        P("dp"),
        P("dp"),
        P("dp", "tensor"),
        P("tensor", "dp"),
        P("tensor", "dp"),
        P("dp"),
        P("dp"),
        P("dp"),
    )
    return jax.shard_map(
        local,
        mesh=mesh,
        in_specs=placed,
        out_specs=(
            P("dp", "tensor"),
            P("dp", "tensor"),
            P(None, "dp", "tensor"),
            P(None, "tensor", "dp"),
            P("tensor", "dp"),
            P("dp"),
            P("dp"),
            P("dp"),
            P("dp", "tensor"),
            P("tensor", "dp"),
            P("tensor", "dp"),
            P("dp"),
            P("dp"),
            P("dp"),
        ),
        check_vma=False,
    )
```

```python
import functools
import math

import jax
import jax.numpy as jnp
from jax import lax
from jax.experimental import pallas as pl
from jax.experimental.pallas import tpu as pltpu
from jax.sharding import PartitionSpec as P

HD = 128


epsilon = 1e-05
neg_large = -1e30
low = jnp.bfloat16
wide = jnp.float32
COST_SCALE = 8


def norm_forward(hidden, gain, shift):
    center = hidden - jnp.mean(hidden, axis=-1, keepdims=True)
    inverse = lax.rsqrt(jnp.mean(center * center, axis=-1, keepdims=True) + epsilon)
    normed = center * inverse
    return (normed * gain + shift, normed, inverse)


def norm_backward(grad_rows, normed, inverse, gain):
    scaled = grad_rows * gain
    mean_first = jnp.mean(scaled, axis=-1, keepdims=True)
    mean_second = jnp.mean(scaled * normed, axis=-1, keepdims=True)
    result = inverse * (scaled - mean_first - normed * mean_second)
    return (result, jnp.sum(grad_rows * normed, axis=0), jnp.sum(grad_rows, axis=0))


def after(array, *others):
    return lax.optimization_barrier((array,) + others)[0] if others else array


def take(array, start, size, axis):
    return lax.dynamic_slice_in_dim(array, start, size, axis)


kernel_params = pltpu.CompilerParams(vmem_limit_bytes=40 * 1024 * 1024)


def product(left, right, left_axis, right_axis):
    dims = (((left_axis,), (right_axis,)), ((), ()))
    return lax.dot_general(left, right, dims, preferred_element_type=wide)


def call(kernel, flops, out_shape, **settings):
    return pl.pallas_call(
        kernel,
        out_shape=out_shape,
        compiler_params=kernel_params,
        cost_estimate=pl.CostEstimate(
            flops=flops // COST_SCALE, bytes_accessed=0, transcendentals=0
        ),
        **settings,
    )


def masked_probs(query, key, valid):
    scores = jnp.where(valid, product(query, key, 1, 1), neg_large)
    expo = jnp.exp((scores - jnp.max(scores, axis=-1, keepdims=True)) * HD ** (-0.5))
    return expo * (1.0 / jnp.sum(expo, axis=-1, keepdims=True))


def valid_keys(length, shift, rows):
    token = lax.broadcasted_iota(jnp.int32, (rows, rows), 1) + shift
    return jnp.where(token < rows, token, token - rows) < length


def attend_kernel(lengths, query, key, value, context):
    rows, features = query.shape
    valid = valid_keys(lengths[pl.program_id(0)], lengths[pl.num_programs(0)], rows)
    for head in range(features // HD):
        at = slice(head * HD, (head + 1) * HD)
        probs = masked_probs(query[:, at], key[:, at], valid)
        context[:, at] = product(probs.astype(low), value[:, at], 1, 0).astype(low)


def attend_back_kernel(lengths, query, key, value, grad, grads):
    rows, features = query.shape
    valid = valid_keys(lengths[pl.program_id(0)], lengths[pl.num_programs(0)], rows)
    for head in range(features // HD):
        at, key_at, value_at = (
            slice(c * features + head * HD, c * features + (head + 1) * HD) for c in range(3)
        )
        probs = masked_probs(query[:, at], key[:, at], valid)
        grads[:, value_at] = product(probs.astype(low), grad[:, at], 0, 0).astype(low)
        prob_grad = product(grad[:, at], value[:, at], 1, 1)
        mean = jnp.sum(prob_grad * probs, axis=-1, keepdims=True)
        score_grad = (probs * (prob_grad - mean)).astype(low)
        grads[:, at] = (product(score_grad, key[:, at], 1, 0) * HD ** (-0.5)).astype(low)
        grads[:, key_at] = (product(score_grad, query[:, at], 0, 0) * HD ** (-0.5)).astype(low)


def by_sequence(kernel, flops, seq_len, lengths, projected, *arrays):
    rows, columns = projected.shape
    features = columns // 3

    def spec(width, block):
        return pl.BlockSpec((seq_len, width), lambda sequence, lengths: (sequence, block))

    size = columns if arrays else features
    return call(
        kernel,
        flops,
        jax.ShapeDtypeStruct((rows, size), low),
        grid_spec=pltpu.PrefetchScalarGridSpec(
            num_scalar_prefetch=1,
            grid=(rows // seq_len,),
            in_specs=[spec(features, c) for c in range(3)] + [spec(features, 0) for a in arrays],
            out_specs=spec(size, 0),
        ),
    )(lengths, projected, projected, projected, *arrays)


def matmul_kernel(right_axis, left, right, *rest):
    total = product(left[...], right[...], 1, right_axis)
    if len(rest) == 2:
        total = total + rest[0][...]
    rest[-1][...] = total.astype(low)


def right_spec(depth, tile, right_axis, start):
    if right_axis:
        return pl.BlockSpec((tile, depth), lambda j: (j, start // depth))
    return pl.BlockSpec((depth, tile), lambda j: (0, start // tile + j))


def column_spec(rows, tile):
    return pl.BlockSpec((rows, tile), lambda j: (0, j))


def matmul(left, right, right_axis, size, start=0, bias=None):
    rows, depth = left.shape
    tile = math.gcd(size, 512 if right_axis or start % 512 == 0 else 256)
    in_specs = [
        pl.BlockSpec((rows, depth), lambda j: (0, 0)),
        right_spec(depth, tile, right_axis, start),
    ]
    operands = [left, right]
    if bias is not None:
        in_specs.append(column_spec(1, tile))
        operands.append(bias[None])
    return call(
        functools.partial(matmul_kernel, right_axis),
        2 * rows * depth * size,
        jax.ShapeDtypeStruct((rows, size), low),
        grid=(size // tile,),
        in_specs=in_specs,
        out_specs=column_spec(rows, tile),
    )(*operands)


def gelu_tanh(values):
    return jnp.tanh((2.0 / math.pi) ** 0.5 * (values + 0.044715 * values * values * values))


def gelu_slope(values):
    tanh = gelu_tanh(values)
    inner = (2.0 / math.pi) ** 0.5 * (1.0 + 3.0 * 0.044715 * values * values)
    return 0.5 * (1.0 + tanh) + 0.5 * values * (1.0 - tanh * tanh) * inner


def up_kernel(rows, weight, bias, pre_act, hidden):
    values = product(rows[...], weight[...], 1, 0) + bias[...]
    pre_act[...] = values
    hidden[...] = (0.5 * values * (1.0 + gelu_tanh(values))).astype(low)


def up_matmul(rows, weight, bias, tile=256):
    count, units = rows.shape[0], bias.shape[0]
    return call(
        up_kernel,
        2 * rows.size * units,
        [
            jax.ShapeDtypeStruct((count, units), wide),
            jax.ShapeDtypeStruct((count, units), low),
        ],
        grid=(units // tile,),
        in_specs=[
            pl.BlockSpec(rows.shape, lambda j: (0, 0)),
            right_spec(rows.shape[1], tile, 0, 0),
            column_spec(1, tile),
        ],
        out_specs=[column_spec(count, tile)] * 2,
    )(rows, weight, bias[None])


def up_back_kernel(grads, weight, slope, pre_grad, bias_grad):
    values = product(grads[...], weight[...], 1, 0) * slope[...].astype(wide)
    rounded = values.astype(low)
    pre_grad[...] = rounded
    bias_grad[...] = jnp.sum(rounded.astype(wide), axis=0, keepdims=True)


def up_back_matmul(grads, weight, slope, tile=256):
    count, units = slope.shape
    return call(
        up_back_kernel,
        2 * grads.size * units,
        [jax.ShapeDtypeStruct((count, units), low), jax.ShapeDtypeStruct((1, units), wide)],
        grid=(units // tile,),
        in_specs=[
            pl.BlockSpec(grads.shape, lambda j: (0, 0)),
            right_spec(grads.shape[1], tile, 0, weight.shape[1] - units),
            column_spec(count, tile),
        ],
        out_specs=[column_spec(count, tile), column_spec(1, tile)],
    )(grads, weight, slope)


def pair_kernel(left_one, right_one, left_two, right_two, total):
    one = product(left_one[...], right_one[...], 0, 0)
    total[...] = (one + product(left_two[...], right_two[...], 0, 0)).astype(low)


def pair_matmul(lefts, rights, tile=256):
    rows, depth = lefts[0].shape
    columns = rights[0].shape[1]
    specs = [column_spec(rows, tile), pl.BlockSpec((rows, columns), lambda j: (0, 0))]
    return call(
        pair_kernel,
        4 * rows * depth * columns,
        jax.ShapeDtypeStruct((depth, columns), low),
        grid=(depth // tile,),
        in_specs=specs * 2,
        out_specs=pl.BlockSpec((tile, columns), lambda j: (j, 0)),
    )(lefts[0], rights[0], lefts[1], rights[1])


def local(
    inputs,
    out_grad,
    lengths,
    dealing,
    qkv_weight,
    qv_bias,
    out_weight,
    out_bias,
    attn_gain,
    attn_shift,
    up_weight,
    up_bias,
    down_weight,
    down_bias,
    ffn_gain,
    ffn_shift,
):
    groups = lax.axis_size("dp")
    ring_size = groups // 4
    index = lax.axis_index("dp")
    core, side, ring = index % 2, (index // 2) % 2, index // 4
    lane = lax.axis_index("tensor")
    core_pairs = [(i, i ^ 1) for i in range(groups)]
    side_pairs = [(i, i ^ 2) for i in range(groups)]
    ring_groups = [[4 * r + offset for r in range(ring_size)] for offset in range(4)]

    def core_swap(array):
        return lax.ppermute(array, "dp", core_pairs)

    def side_swap(array):
        return lax.ppermute(array, "dp", side_pairs)

    def lane_swap(array):
        return lax.ppermute(array, "tensor", [(0, 1), (1, 0)])

    def in_order(bit, mine, theirs, axis):
        first = jnp.where(bit == 0, mine, theirs)
        second = jnp.where(bit == 0, theirs, mine)
        return jnp.concatenate([first, second], axis=axis)

    def parts(array, bit, axis):
        size = array.shape[axis] // 2
        return take(array, bit * size, size, axis), take(array, (1 - bit) * size, size, axis)

    seq_len, half = inputs.shape
    width = 2 * half
    per_peer = seq_len // groups
    shard = width // groups
    token_half = seq_len // 2
    features = half // 4
    units = up_weight.shape[1] // 4

    def split_weight(weight):
        mine, sent = parts(weight, core, 2)
        weight = in_order(core, mine, core_swap(sent), 0)
        mine, sent = parts(weight, side, 2)
        weight = in_order(side, mine, side_swap(sent), 0)
        return weight.reshape(4 * shard, -1)

    def gather_weight(piece):
        return lax.all_gather(piece, "dp", axis=0, axis_index_groups=ring_groups, tiled=True)

    first_weights = jnp.concatenate([qkv_weight, out_weight.T[None]], axis=0).swapaxes(0, 1)
    first_piece = split_weight(first_weights)
    first_full = gather_weight(first_piece)
    second_weights = after(up_weight, first_piece), after(down_weight, first_piece).T
    second_piece = split_weight(jnp.stack(second_weights, axis=1))
    second_full = gather_weight(second_piece)

    local_rows = inputs.reshape(groups, per_peer, half).swapaxes(0, 1)
    sending = jnp.take(local_rows, dealing, axis=1)
    arrived = lax.all_to_all(sending, "dp", split_axis=1, concat_axis=1, tiled=True)
    tokens = after(arrived, first_piece).reshape(seq_len, half)
    early, late = tokens[:token_half], tokens[token_half:]
    early = in_order(lane, early, lane_swap(early), 1)
    early = jnp.stack([early, side_swap(early)])
    late = jnp.stack([late, side_swap(late)])
    late = in_order(lane, late, lane_swap(late), 2)
    own_rows = jnp.stack([jnp.where(lane == 0, early, late), jnp.where(lane == 0, late, early)], 1)
    own_rows = own_rows.reshape(2 * seq_len, width)
    all_rows = (own_rows, core_swap(own_rows))
    residual = own_rows[:token_half]
    grad_keep, grad_send = parts(out_grad, lane, 0)
    cotangent = in_order(lane, grad_keep, lane_swap(grad_send), 1)

    small = jnp.concatenate(
        [
            v.reshape(-1)
            for v in (
                qv_bias,
                up_bias,
                out_bias,
                attn_gain,
                attn_shift,
                down_bias,
                ffn_gain,
                ffn_shift,
            )
        ]
    )[None]
    small = in_order(core, small, core_swap(after(small, first_piece)), 0)
    small = in_order(side, small, side_swap(small), 0)
    small_all = jnp.zeros((groups, small.shape[1]), low)
    for step in range(ring_size):
        if step:
            small = lax.ppermute(small, "dp", [(i, (i + 4) % groups) for i in range(groups)])
        place = ((ring - step) % ring_size) * 4
        small_all = lax.dynamic_update_slice_in_dim(small_all, small, place, 0)
    cut_one = qv_bias.size
    cut_two = cut_one + up_bias.size
    qv_full = (
        small_all[:, :cut_one]
        .reshape((groups,) + qv_bias.shape)
        .transpose(1, 2, 0, 3)
        .reshape(2, half)
    )
    up_bias_full = (
        small_all[:, cut_one:cut_two]
        .reshape((groups,) + up_bias.shape)
        .transpose(1, 0, 2)
        .reshape(-1)
    )
    vectors = (
        small_all[:, cut_two:].reshape(groups, 6, shard).transpose(1, 0, 2).reshape(6, width)
    ).astype(wide)
    out_bias_full, gain_one, shift_one, down_bias_full, gain_two, shift_two = vectors
    place = core * 2 + side
    qv_rows = take(qv_full, place * features, features, 1)
    up_bias_mine = take(up_bias_full, place * units, units, 0)

    def core_parts(left, right, start=0):
        theirs = core_swap(matmul(left[1], right, 1, width, start))
        mine = matmul(left[0], right, 1, width, start)
        return mine, theirs

    def added(both, pick):
        mine, theirs = (pick(array.reshape(2, 2, token_half, width)) for array in both)
        return mine.astype(wide) + theirs.astype(wide)

    def group_sum(both, beside_one=(), beside_two=()):
        one = side_swap(added(both, lambda a: a[1, ..., :half]).astype(low))
        two = lane_swap(added(both, lambda a: a[:, 1, :, half:]).astype(low))
        one = added(both, lambda a: a[0, ..., :half]) + after(one, *beside_one).astype(wide)
        two = added(both, lambda a: a[:, 0, :, half:]) + after(two, *beside_one).astype(wide)
        one = one[0] + after(lane_swap(one[1].astype(low)), *beside_two).astype(wide)
        two = two[0] + after(side_swap(two[1].astype(low)), *beside_two).astype(wide)
        return jnp.concatenate([one, two], axis=1)

    def group_gather(rows, beside_one=(), beside_two=()):
        one, two = rows[:, :half], rows[:, half:]
        one = jnp.stack([one, after(lane_swap(one), *beside_one)])
        two = jnp.stack([two, after(side_swap(two), *beside_one)])
        one = jnp.stack([one, after(side_swap(one), *beside_two)])
        two = jnp.stack([two, after(lane_swap(two), *beside_two)], axis=1)
        own = jnp.concatenate([one, two], axis=3).reshape(2 * seq_len, width)
        return own, core_swap(own)

    sequences = jnp.stack([index, index ^ 2, index ^ 1, index ^ 3])
    group_lengths = jnp.take(lengths, jnp.take(dealing, sequences)).reshape(2, 2)
    group_lengths = jnp.concatenate(
        [group_lengths, jnp.full((2, 1), lane * token_half, jnp.int32)], axis=1
    )
    qkv_bias = jnp.concatenate([qv_rows[0], jnp.zeros_like(qv_rows[0]), qv_rows[1]]).astype(wide)
    flops = 4 * 2 * seq_len * seq_len * features
    all_rows = tuple(after(rows, second_piece) for rows in all_rows)
    projected = [matmul(rows, first_full, 0, 3 * features, bias=qkv_bias) for rows in all_rows]
    context = [
        by_sequence(attend_kernel, 4 * flops, seq_len, group_lengths[i], projected[i])
        for i in range(2)
    ]
    attended = group_sum(core_parts(context, first_full, 3 * features)) + out_bias_full
    first, normed_one, inverse_one = norm_forward(
        residual.astype(wide) + attended, gain_one, shift_one
    )
    first_low = group_gather(first.astype(low))

    pre_act, hidden = zip(
        *[up_matmul(rows, second_full, up_bias_mine.astype(wide)) for rows in first_low], strict=True
    )
    mixed_parts = core_parts(hidden, second_full, units)
    slope = [gelu_slope(after(values, *mixed_parts)).astype(low) for values in pre_act]
    mixed = group_sum(mixed_parts, slope) + down_bias_full
    final, normed_two, inverse_two = norm_forward(first + mixed, gain_two, shift_two)
    second_grad, gain_two_grad, shift_two_grad = norm_backward(
        cotangent.astype(wide), normed_two, inverse_two, gain_two
    )
    mixed_low = second_grad.astype(low)
    down_bias_grad = jnp.sum(mixed_low, axis=0, dtype=wide)
    mixed_grad = group_gather(mixed_low)

    def scatter(partial):
        return lax.psum_scatter(
            partial, "dp", scatter_dimension=0, axis_index_groups=ring_groups, tiled=True
        )

    def join_grad(total, kinds):
        total = total.reshape(4 * shard, kinds, -1)
        mine, sent = parts(total, side, 0)
        total = in_order(side, mine, side_swap(sent), 2)
        mine, sent = parts(total, core, 0)
        return in_order(core, mine, core_swap(sent), 2).astype(wide)

    down_partial = pair_matmul(mixed_grad, hidden)
    down_sum = scatter(down_partial)
    pre_grad, up_bias_grad = zip(
        *[
            up_back_matmul(after(mixed_grad[i], down_partial), second_full, slope[i])
            for i in range(2)
        ],
        strict=True,
    )
    both = core_parts(pre_grad, second_full)
    up_partial = pair_matmul(first_low, [after(grads, *both) for grads in pre_grad])
    up_sum = scatter(up_partial)
    first_grad = second_grad + group_sum(both, [up_partial], [down_sum])
    attn_total_grad, gain_one_grad, shift_one_grad = norm_backward(
        first_grad, normed_one, inverse_one, gain_one
    )
    attended_low = attn_total_grad.astype(low)
    out_bias_grad = jnp.sum(attended_low, axis=0, dtype=wide)
    attended_grad = group_gather(attended_low)
    out_partial = pair_matmul(attended_grad, context)
    out_sum = scatter(out_partial)
    context_grad = [
        matmul(after(rows, out_partial), first_full, 0, features, 3 * features)
        for rows in attended_grad
    ]
    stacked = [
        by_sequence(
            attend_back_kernel,
            8 * flops,
            seq_len,
            group_lengths[i],
            projected[i],
            context_grad[i],
        )
        for i in range(2)
    ]
    both = core_parts((stacked[0], after(stacked[1], up_sum)), first_full)
    own_part = sum(array.astype(wide) for array in both).astype(low)
    own_part = own_part.reshape(2, 2, token_half, width)
    early, late = (
        jnp.where(lane == bit, own_part[:, 0], own_part[:, 1]) for bit in range(2)
    )
    early_sent = early[1]
    late, late_sent = parts(late, lane, 2)
    qkv_partial = pair_matmul(all_rows, [after(g, early_sent, late_sent) for g in stacked])
    qkv_sum = scatter(qkv_partial)
    early = early[0].astype(wide) + side_swap(early_sent).astype(wide)
    late = late.astype(wide) + after(lane_swap(late_sent), qkv_partial).astype(wide)
    early, early_sent = parts(early, lane, 1)
    early_sent, late_sent = early_sent.astype(low), late[1].astype(low)
    early = early + lane_swap(early_sent).astype(wide)
    late = late[0] + side_swap(late_sent).astype(wide)
    own_attended = take(attended_grad[0][:seq_len], lane * half, half, 1)
    own_attended = in_order(lane, own_attended[:token_half], own_attended[token_half:], 0)
    in_half = (jnp.concatenate([early, late], axis=0) + own_attended.astype(wide)).astype(low)
    qkv_bias_sum = sum(jnp.sum(after(s, early_sent), axis=0, dtype=wide) for s in stacked)
    qkv_bias_sum = qkv_bias_sum.reshape(3, features)
    qv_grad = jnp.stack([qkv_bias_sum[0], qkv_bias_sum[2]])
    out_keep, out_send = parts(final.astype(low), lane, 1)
    outputs = in_order(lane, out_keep, lane_swap(after(out_send, early_sent)), 0)

    back_rows = in_half.reshape(per_peer, groups, half)
    returned = lax.all_to_all(back_rows, "dp", split_axis=1, concat_axis=1, tiled=True)
    inverse_order = (
        jnp.zeros((groups,), jnp.int32).at[dealing].set(jnp.arange(groups, dtype=jnp.int32))
    )
    in_grad = jnp.take(returned, inverse_order, axis=1).swapaxes(0, 1).reshape(seq_len, half)

    down_weight_grad = join_grad(after(down_sum, qkv_partial), 1)[:, 0].T
    up_weight_grad = join_grad(after(up_sum, qkv_partial), 1)[:, 0]
    out_weight_grad = join_grad(after(out_sum, early_sent), 1)[:, 0].T
    qkv_grad = join_grad(qkv_sum, 3).swapaxes(0, 1)

    def spread(mine, size):
        full = jnp.zeros(mine.shape[:-1] + (4 * size,), wide)
        return lax.dynamic_update_slice_in_dim(full, mine, place * size, mine.ndim - 1)

    qv_spread = (
        spread(qv_grad, features)
        .reshape(2, qv_bias.shape[1], groups, qv_bias.shape[2])
        .transpose(2, 0, 1, 3)
        .reshape(groups, -1)
    )
    up_spread = (
        spread((up_bias_grad[0] + up_bias_grad[1])[0], units)
        .reshape(up_bias.shape[0], groups, up_bias.shape[1])
        .transpose(1, 0, 2)
        .reshape(groups, -1)
    )
    vector_spread = (
        jnp.stack(
            [
                out_bias_grad,
                gain_one_grad,
                shift_one_grad,
                down_bias_grad,
                gain_two_grad,
                shift_two_grad,
            ]
        )
        .reshape(6, groups, shard)
        .transpose(1, 0, 2)
        .reshape(groups, -1)
    )
    packed = jnp.concatenate([qv_spread, up_spread, vector_spread], axis=1)
    exchanged = lax.all_to_all(packed, "dp", split_axis=0, concat_axis=0, tiled=True)
    small_sum = jnp.sum(exchanged, axis=0)
    vector_sum = small_sum[cut_two:]
    vector_sum = (vector_sum + lane_swap(vector_sum)).reshape(6, shard)
    return (
        outputs,
        in_grad,
        qkv_grad,
        small_sum[:cut_one].reshape(qv_bias.shape),
        out_weight_grad,
        vector_sum[0],
        vector_sum[1],
        vector_sum[2],
        up_weight_grad,
        small_sum[cut_one:cut_two].reshape(up_bias.shape),
        down_weight_grad,
        vector_sum[3],
        vector_sum[4],
        vector_sum[5],
    )


def solution(mesh):
    placed = (
        P("dp", "tensor"),
        P("dp", "tensor"),
        P(),
        P(),
        P(None, "dp", "tensor"),
        P(None, "tensor", "dp"),
        P("tensor", "dp"),
        P("dp"),
        P("dp"),
        P("dp"),
        P("dp", "tensor"),
        P("tensor", "dp"),
        P("tensor", "dp"),
        P("dp"),
        P("dp"),
        P("dp"),
    )
    return jax.shard_map(
        local,
        mesh=mesh,
        in_specs=placed,
        out_specs=(
            P("dp", "tensor"),
            P("dp", "tensor"),
            P(None, "dp", "tensor"),
            P(None, "tensor", "dp"),
            P("tensor", "dp"),
            P("dp"),
            P("dp"),
            P("dp"),
            P("dp", "tensor"),
            P("tensor", "dp"),
            P("tensor", "dp"),
            P("dp"),
            P("dp"),
            P("dp"),
        ),
        check_vma=False,
    )
```

```python
import functools
import math

import jax
import jax.numpy as jnp
from jax import lax
from jax.experimental import pallas as pl
from jax.experimental.pallas import tpu as pltpu
from jax.sharding import PartitionSpec as P

HD = 128


epsilon = 1e-05
neg_large = -1e30
low = jnp.bfloat16
wide = jnp.float32
COST_SCALE = 8


def norm_forward(hidden, gain, shift):
    center = hidden - jnp.mean(hidden, axis=-1, keepdims=True)
    inverse = lax.rsqrt(jnp.mean(center * center, axis=-1, keepdims=True) + epsilon)
    normed = center * inverse
    return (normed * gain + shift, normed, inverse)


def norm_backward(grad_rows, normed, inverse, gain):
    scaled = grad_rows * gain
    mean_first = jnp.mean(scaled, axis=-1, keepdims=True)
    mean_second = jnp.mean(scaled * normed, axis=-1, keepdims=True)
    result = inverse * (scaled - mean_first - normed * mean_second)
    return (result, jnp.sum(grad_rows * normed, axis=0), jnp.sum(grad_rows, axis=0))


def after(array, *others):
    return lax.optimization_barrier((array,) + others)[0] if others else array


def take(array, start, size, axis):
    return lax.dynamic_slice_in_dim(array, start, size, axis)


kernel_params = pltpu.CompilerParams(vmem_limit_bytes=40 * 1024 * 1024)


def product(left, right, left_axis, right_axis):
    dims = (((left_axis,), (right_axis,)), ((), ()))
    return lax.dot_general(left, right, dims, preferred_element_type=wide)


def call(kernel, flops, out_shape, **settings):
    return pl.pallas_call(
        kernel,
        out_shape=out_shape,
        compiler_params=kernel_params,
        cost_estimate=pl.CostEstimate(
            flops=flops // COST_SCALE, bytes_accessed=0, transcendentals=0
        ),
        **settings,
    )


def masked_probs(query, key, valid):
    scores = jnp.where(valid, product(query, key, 1, 1), neg_large)
    expo = jnp.exp((scores - jnp.max(scores, axis=-1, keepdims=True)) * HD ** (-0.5))
    return expo * (1.0 / jnp.sum(expo, axis=-1, keepdims=True))


def valid_keys(length, shift, rows):
    token = lax.broadcasted_iota(jnp.int32, (rows, rows), 1) + shift
    return jnp.where(token < rows, token, token - rows) < length


def attend_kernel(lengths, query, key, value, context):
    rows, features = query.shape
    valid = valid_keys(lengths[pl.program_id(0)], lengths[pl.num_programs(0)], rows)
    for head in range(features // HD):
        at = slice(head * HD, (head + 1) * HD)
        probs = masked_probs(query[:, at], key[:, at], valid)
        context[:, at] = product(probs.astype(low), value[:, at], 1, 0).astype(low)


def attend_back_kernel(lengths, query, key, value, grad, grads):
    rows, features = query.shape
    valid = valid_keys(lengths[pl.program_id(0)], lengths[pl.num_programs(0)], rows)
    for head in range(features // HD):
        at, key_at, value_at = (
            slice(c * features + head * HD, c * features + (head + 1) * HD) for c in range(3)
        )
        probs = masked_probs(query[:, at], key[:, at], valid)
        grads[:, value_at] = product(probs.astype(low), grad[:, at], 0, 0).astype(low)
        prob_grad = product(grad[:, at], value[:, at], 1, 1)
        mean = jnp.sum(prob_grad * probs, axis=-1, keepdims=True)
        score_grad = (probs * (prob_grad - mean)).astype(low)
        grads[:, at] = (product(score_grad, key[:, at], 1, 0) * HD ** (-0.5)).astype(low)
        grads[:, key_at] = (product(score_grad, query[:, at], 0, 0) * HD ** (-0.5)).astype(low)


def by_sequence(kernel, flops, seq_len, lengths, projected, *arrays):
    rows, columns = projected.shape
    features = columns // 3

    def spec(width, block):
        return pl.BlockSpec((seq_len, width), lambda sequence, lengths: (sequence, block))

    size = columns if arrays else features
    return call(
        kernel,
        flops,
        jax.ShapeDtypeStruct((rows, size), low),
        grid_spec=pltpu.PrefetchScalarGridSpec(
            num_scalar_prefetch=1,
            grid=(rows // seq_len,),
            in_specs=[spec(features, c) for c in range(3)] + [spec(features, 0) for a in arrays],
            out_specs=spec(size, 0),
        ),
    )(lengths, projected, projected, projected, *arrays)


def matmul_kernel(right_axis, left, right, *rest):
    total = product(left[...], right[...], 1, right_axis)
    if len(rest) == 2:
        total = total + rest[0][...]
    rest[-1][...] = total.astype(low)


def right_spec(depth, tile, right_axis, start):
    if right_axis:
        return pl.BlockSpec((tile, depth), lambda j: (j, start // depth))
    return pl.BlockSpec((depth, tile), lambda j: (0, start // tile + j))


def column_spec(rows, tile):
    return pl.BlockSpec((rows, tile), lambda j: (0, j))


def matmul(left, right, right_axis, size, start=0, bias=None):
    rows, depth = left.shape
    tile = math.gcd(size, 512 if right_axis or start % 512 == 0 else 256)
    in_specs = [
        pl.BlockSpec((rows, depth), lambda j: (0, 0)),
        right_spec(depth, tile, right_axis, start),
    ]
    operands = [left, right]
    if bias is not None:
        in_specs.append(column_spec(1, tile))
        operands.append(bias[None])
    return call(
        functools.partial(matmul_kernel, right_axis),
        2 * rows * depth * size,
        jax.ShapeDtypeStruct((rows, size), low),
        grid=(size // tile,),
        in_specs=in_specs,
        out_specs=column_spec(rows, tile),
    )(*operands)


def gelu_tanh(values):
    return jnp.tanh((2.0 / math.pi) ** 0.5 * (values + 0.044715 * values * values * values))


def gelu_slope(values):
    tanh = gelu_tanh(values)
    inner = (2.0 / math.pi) ** 0.5 * (1.0 + 3.0 * 0.044715 * values * values)
    return 0.5 * (1.0 + tanh) + 0.5 * values * (1.0 - tanh * tanh) * inner


def up_kernel(rows, weight, bias, pre_act, hidden):
    values = product(rows[...], weight[...], 1, 0) + bias[...]
    pre_act[...] = values
    hidden[...] = (0.5 * values * (1.0 + gelu_tanh(values))).astype(low)


def up_matmul(rows, weight, bias, tile=256):
    count, units = rows.shape[0], bias.shape[0]
    return call(
        up_kernel,
        2 * rows.size * units,
        [
            jax.ShapeDtypeStruct((count, units), wide),
            jax.ShapeDtypeStruct((count, units), low),
        ],
        grid=(units // tile,),
        in_specs=[
            pl.BlockSpec(rows.shape, lambda j: (0, 0)),
            right_spec(rows.shape[1], tile, 0, 0),
            column_spec(1, tile),
        ],
        out_specs=[column_spec(count, tile)] * 2,
    )(rows, weight, bias[None])


def up_back_kernel(grads, weight, slope, pre_grad, bias_grad):
    values = product(grads[...], weight[...], 1, 0) * slope[...].astype(wide)
    rounded = values.astype(low)
    pre_grad[...] = rounded
    bias_grad[...] = jnp.sum(rounded.astype(wide), axis=0, keepdims=True)


def up_back_matmul(grads, weight, slope, tile=256):
    count, units = slope.shape
    return call(
        up_back_kernel,
        2 * grads.size * units,
        [jax.ShapeDtypeStruct((count, units), low), jax.ShapeDtypeStruct((1, units), wide)],
        grid=(units // tile,),
        in_specs=[
            pl.BlockSpec(grads.shape, lambda j: (0, 0)),
            right_spec(grads.shape[1], tile, 0, weight.shape[1] - units),
            column_spec(count, tile),
        ],
        out_specs=[column_spec(count, tile), column_spec(1, tile)],
    )(grads, weight, slope)


def pair_kernel(left_one, right_one, left_two, right_two, total):
    one = product(left_one[...], right_one[...], 0, 0)
    total[...] = (one + product(left_two[...], right_two[...], 0, 0)).astype(low)


def pair_matmul(lefts, rights, tile=256):
    rows, depth = lefts[0].shape
    columns = rights[0].shape[1]
    specs = [column_spec(rows, tile), pl.BlockSpec((rows, columns), lambda j: (0, 0))]
    return call(
        pair_kernel,
        4 * rows * depth * columns,
        jax.ShapeDtypeStruct((depth, columns), low),
        grid=(depth // tile,),
        in_specs=specs * 2,
        out_specs=pl.BlockSpec((tile, columns), lambda j: (j, 0)),
    )(lefts[0], rights[0], lefts[1], rights[1])


def local(
    inputs,
    out_grad,
    lengths,
    dealing,
    qkv_weight,
    qv_bias,
    out_weight,
    out_bias,
    attn_gain,
    attn_shift,
    up_weight,
    up_bias,
    down_weight,
    down_bias,
    ffn_gain,
    ffn_shift,
):
    groups = lax.axis_size("dp")
    ring_size = groups // 4
    index = lax.axis_index("dp")
    core, side, ring = index % 2, (index // 2) % 2, index // 4
    lane = lax.axis_index("tensor")
    core_pairs = [(i, i ^ 1) for i in range(groups)]
    side_pairs = [(i, i ^ 2) for i in range(groups)]
    ring_groups = [[4 * r + offset for r in range(ring_size)] for offset in range(4)]

    def core_swap(array):
        return lax.ppermute(array, "dp", core_pairs)

    def side_swap(array):
        return lax.ppermute(array, "dp", side_pairs)

    def ring_send(array, steps):
        return lax.ppermute(array, "dp", [(i, (i + 4 * steps) % groups) for i in range(groups)])

    def lane_swap(array):
        return lax.ppermute(array, "tensor", [(0, 1), (1, 0)])

    def in_order(bit, mine, theirs, axis):
        first = jnp.where(bit == 0, mine, theirs)
        second = jnp.where(bit == 0, theirs, mine)
        return jnp.concatenate([first, second], axis=axis)

    def parts(array, bit, axis):
        size = array.shape[axis] // 2
        return take(array, bit * size, size, axis), take(array, (1 - bit) * size, size, axis)

    seq_len, half = inputs.shape
    width = 2 * half
    per_peer = seq_len // groups
    shard = width // groups
    token_half = seq_len // 2
    features = half // 4
    units = up_weight.shape[1] // 4

    def split_weight(weight):
        mine, sent = parts(weight, core, 2)
        weight = in_order(core, mine, core_swap(sent), 0)
        mine, sent = parts(weight, side, 2)
        weight = in_order(side, mine, side_swap(sent), 0)
        return weight.reshape(4 * shard, -1)

    def gather_weight(piece):
        return lax.all_gather(piece, "dp", axis=0, axis_index_groups=ring_groups, tiled=True)

    first_weights = jnp.concatenate([qkv_weight, out_weight.T[None]], axis=0).swapaxes(0, 1)
    first_piece = split_weight(first_weights)
    first_full = gather_weight(first_piece)
    second_weights = after(up_weight, first_piece), after(down_weight, first_piece).T
    second_piece = split_weight(jnp.stack(second_weights, axis=1))
    second_full = gather_weight(second_piece)

    small = jnp.concatenate(
        [
            v.reshape(-1)
            for v in (
                qv_bias,
                up_bias,
                out_bias,
                attn_gain,
                attn_shift,
                down_bias,
                ffn_gain,
                ffn_shift,
            )
        ]
    )[None]
    small = in_order(core, small, core_swap(after(small, first_piece)), 0)
    small = in_order(side, small, side_swap(small), 0)
    small_all = lax.dynamic_update_slice_in_dim(
        jnp.zeros((groups, small.shape[1]), low), small, ring * 4, 0
    )
    for step in range(1, ring_size):
        place = ((ring - step) % ring_size) * 4
        small_all = lax.dynamic_update_slice_in_dim(small_all, ring_send(small, step), place, 0)

    local_rows = inputs.reshape(groups, per_peer, half).swapaxes(0, 1)
    sending = jnp.take(local_rows, dealing, axis=1)
    arrived = lax.all_to_all(sending, "dp", split_axis=1, concat_axis=1, tiled=True)
    tokens = after(arrived, first_piece).reshape(seq_len, half)
    early, late = tokens[:token_half], tokens[token_half:]
    early = in_order(lane, early, lane_swap(early), 1)
    early = jnp.stack([early, side_swap(early)])
    late = jnp.stack([late, side_swap(late)])
    late = in_order(lane, late, lane_swap(late), 2)
    own_rows = jnp.stack([jnp.where(lane == 0, early, late), jnp.where(lane == 0, late, early)], 1)
    own_rows = after(own_rows.reshape(2 * seq_len, width), second_piece, small_all)
    all_rows = (own_rows, core_swap(own_rows))
    residual = own_rows[:token_half]
    grad_keep, grad_send = parts(out_grad, lane, 0)
    cotangent = in_order(lane, grad_keep, lane_swap(grad_send), 1)

    cut_one = qv_bias.size
    cut_two = cut_one + up_bias.size
    qv_full = (
        small_all[:, :cut_one]
        .reshape((groups,) + qv_bias.shape)
        .transpose(1, 2, 0, 3)
        .reshape(2, half)
    )
    up_bias_full = (
        small_all[:, cut_one:cut_two]
        .reshape((groups,) + up_bias.shape)
        .transpose(1, 0, 2)
        .reshape(-1)
    )
    vectors = (
        small_all[:, cut_two:].reshape(groups, 6, shard).transpose(1, 0, 2).reshape(6, width)
    ).astype(wide)
    out_bias_full, gain_one, shift_one, down_bias_full, gain_two, shift_two = vectors
    place = core * 2 + side
    qv_rows = take(qv_full, place * features, features, 1)
    up_bias_mine = take(up_bias_full, place * units, units, 0)

    def core_parts(left, right, start=0):
        theirs = core_swap(matmul(left[1], right, 1, width, start))
        mine = matmul(left[0], right, 1, width, start)
        return mine, theirs

    def added(both, pick):
        mine, theirs = (pick(array.reshape(2, 2, token_half, width)) for array in both)
        return mine.astype(wide) + theirs.astype(wide)

    def group_sum(both, beside_one=(), beside_two=()):
        one = side_swap(added(both, lambda a: a[1, ..., :half]).astype(low))
        two = lane_swap(added(both, lambda a: a[:, 1, :, half:]).astype(low))
        one = added(both, lambda a: a[0, ..., :half]) + after(one, *beside_one).astype(wide)
        two = added(both, lambda a: a[:, 0, :, half:]) + after(two, *beside_one).astype(wide)
        one = one[0] + after(lane_swap(one[1].astype(low)), *beside_two).astype(wide)
        two = two[0] + after(side_swap(two[1].astype(low)), *beside_two).astype(wide)
        return jnp.concatenate([one, two], axis=1)

    def group_gather(rows, beside_own=()):
        one, two = rows[:, :half], rows[:, half:]
        one = jnp.stack([one, lane_swap(one)])
        two = jnp.stack([two, side_swap(two)])
        one = jnp.stack([one, side_swap(one)])
        two = jnp.stack([two, lane_swap(two)], axis=1)
        own = jnp.concatenate([one, two], axis=3).reshape(2 * seq_len, width)
        own = after(own, *beside_own)
        return own, core_swap(own)

    sequences = jnp.stack([index, index ^ 2, index ^ 1, index ^ 3])
    group_lengths = jnp.take(lengths, jnp.take(dealing, sequences)).reshape(2, 2)
    group_lengths = jnp.concatenate(
        [group_lengths, jnp.full((2, 1), lane * token_half, jnp.int32)], axis=1
    )
    qkv_bias = jnp.concatenate([qv_rows[0], jnp.zeros_like(qv_rows[0]), qv_rows[1]]).astype(wide)
    flops = 4 * 2 * seq_len * seq_len * features
    projected, context = [], []
    for i in range(2):
        rows = after(all_rows[i], *context)
        projected.append(matmul(rows, first_full, 0, 3 * features, bias=qkv_bias))
        context.append(
            by_sequence(attend_kernel, 4 * flops, seq_len, group_lengths[i], projected[i])
        )
    attended = group_sum(core_parts(context, first_full, 3 * features)) + out_bias_full
    first, normed_one, inverse_one = norm_forward(
        residual.astype(wide) + attended, gain_one, shift_one
    )
    first_low = group_gather(first.astype(low), [second_full])

    pre_act, hidden = [], []
    for i in range(2):
        values, outs = up_matmul(after(first_low[i], *hidden), second_full, up_bias_mine.astype(wide))
        pre_act.append(values)
        hidden.append(outs)
    mixed_parts = core_parts(hidden, second_full, units)
    slope = [gelu_slope(after(values, *mixed_parts)).astype(low) for values in pre_act]
    mixed = group_sum(mixed_parts, slope) + down_bias_full
    final, normed_two, inverse_two = norm_forward(first + mixed, gain_two, shift_two)
    second_grad, gain_two_grad, shift_two_grad = norm_backward(
        cotangent.astype(wide), normed_two, inverse_two, gain_two
    )
    mixed_low = second_grad.astype(low)
    down_bias_grad = jnp.sum(mixed_low, axis=0, dtype=wide)
    mixed_grad = group_gather(mixed_low)

    def scatter(partial):
        return lax.psum_scatter(
            partial, "dp", scatter_dimension=0, axis_index_groups=ring_groups, tiled=True
        )

    def side_send(total, kinds):
        total = total.reshape(4 * shard, kinds, -1)
        mine, sent = parts(total, side, 0)
        return mine, side_swap(sent)

    def side_join(mine, theirs):
        return in_order(side, mine, theirs, 2)

    def core_join(total):
        mine, sent = parts(total, core, 0)
        return in_order(core, mine, core_swap(sent), 2).astype(wide)

    pre_grad = [up_back_matmul(mixed_grad[0], second_full, slope[0])]
    mixed_grad = (mixed_grad[0], after(mixed_grad[1], pre_grad[0][0]))
    down_partial = pair_matmul(mixed_grad, hidden)
    down_sum = scatter(down_partial)
    pre_grad.append(up_back_matmul(after(mixed_grad[1], down_partial), second_full, slope[1]))
    pre_grad, up_bias_grad = zip(*pre_grad, strict=True)
    both = core_parts(pre_grad, second_full)
    up_partial = pair_matmul(first_low, [after(grads, *both) for grads in pre_grad])
    up_sum = scatter(up_partial)
    first_grad = second_grad + group_sum(both, [up_partial], [down_sum])
    attn_total_grad, gain_one_grad, shift_one_grad = norm_backward(
        first_grad, normed_one, inverse_one, gain_one
    )
    attended_low = attn_total_grad.astype(low)
    out_bias_grad = jnp.sum(attended_low, axis=0, dtype=wide)
    attended_grad = group_gather(attended_low)
    down_sum = side_send(down_sum, 1)
    stacked = []
    for i in range(2):
        rows = attended_grad[i]
        if i:
            attended_grad = (attended_grad[0], after(rows, *stacked, down_sum[1]))
            out_partial = pair_matmul(attended_grad, context)
            out_sum = scatter(out_partial)
            rows = after(attended_grad[1], out_partial)
        context_grad = matmul(rows, first_full, 0, features, 3 * features)
        stacked.append(
            by_sequence(
                attend_back_kernel,
                8 * flops,
                seq_len,
                group_lengths[i],
                projected[i],
                context_grad,
            )
        )
    theirs = matmul(after(stacked[1], up_sum), first_full, 1, width)
    qkv_partial = pair_matmul(all_rows, [after(grads, theirs) for grads in stacked])
    qkv_sum = scatter(qkv_partial)
    theirs = core_swap(theirs)
    mine = matmul(after(stacked[0], qkv_partial), first_full, 1, width)
    up_sum = side_send(up_sum, 1)

    quarter = half // 2
    both = tuple(array.reshape(2, seq_len, width) for array in (after(mine, up_sum[1]), theirs))

    def summed(pick):
        return sum(pick(array).astype(wide) for array in both)

    def across(array):
        return jnp.concatenate([array[..., :quarter], array[..., half : half + quarter]], axis=-1)

    def of_lane(bit):
        return lambda array: take(array, bit * half + quarter, quarter, 2)

    def lane_swap_rows(array):
        array = lane_swap(array)
        return jnp.concatenate([array[..., token_half:, :], array[..., :token_half, :]], axis=-2)

    one_sent = summed(lambda array: across(array[1])).astype(low)
    two_sent = summed(of_lane(1 - lane)).astype(low)
    one, two = side_swap(one_sent), lane_swap_rows(two_sent)
    one = summed(lambda array: across(array[0])) + one.astype(wide)
    two = summed(of_lane(lane)) + two.astype(wide)
    one_sent = take(one, (1 - lane) * quarter, quarter, 1).astype(low)
    two_sent = two[1].astype(low)
    one = take(one, lane * quarter, quarter, 1) + lane_swap_rows(one_sent).astype(wide)
    two = two[0] + side_swap(two_sent).astype(wide)
    own_attended = take(attended_grad[0][:seq_len], lane * half, half, 1)
    in_half = (jnp.concatenate([one, two], axis=1) + own_attended.astype(wide)).astype(low)
    in_half = in_order(lane, in_half[:token_half], in_half[token_half:], 0)
    down_weight_grad = core_join(after(side_join(*down_sum), one_sent))[:, 0].T
    up_weight_grad = core_join(after(side_join(*up_sum), one_sent))[:, 0]
    in_half = after(in_half, down_weight_grad, up_weight_grad)
    back_rows = in_half.reshape(per_peer, groups, half)
    out_keep, out_send = parts(final.astype(low), lane, 1)
    outputs = in_order(lane, out_keep, lane_swap(after(out_send, back_rows)), 0)
    qkv_bias_sum = sum(jnp.sum(after(s, back_rows), axis=0, dtype=wide) for s in stacked)
    qkv_bias_sum = qkv_bias_sum.reshape(3, features)
    qv_grad = jnp.stack([qkv_bias_sum[0], qkv_bias_sum[2]])
    def spread(mine, size):
        full = jnp.zeros(mine.shape[:-1] + (4 * size,), wide)
        return lax.dynamic_update_slice_in_dim(full, mine, place * size, mine.ndim - 1)

    qv_spread = (
        spread(qv_grad, features)
        .reshape(2, qv_bias.shape[1], groups, qv_bias.shape[2])
        .transpose(2, 0, 1, 3)
        .reshape(groups, -1)
    )
    up_spread = (
        spread((up_bias_grad[0] + up_bias_grad[1])[0], units)
        .reshape(up_bias.shape[0], groups, up_bias.shape[1])
        .transpose(1, 0, 2)
        .reshape(groups, -1)
    )
    vector_spread = (
        jnp.stack(
            [
                out_bias_grad,
                gain_one_grad,
                shift_one_grad,
                down_bias_grad,
                gain_two_grad,
                shift_two_grad,
            ]
        )
        .reshape(6, groups, shard)
        .transpose(1, 0, 2)
        .reshape(groups, -1)
    )
    packed = jnp.concatenate([qv_spread, up_spread, vector_spread], axis=1)
    packed = after(packed, back_rows)

    returned = lax.all_to_all(back_rows, "dp", split_axis=1, concat_axis=1, tiled=True)
    inverse_order = (
        jnp.zeros((groups,), jnp.int32).at[dealing].set(jnp.arange(groups, dtype=jnp.int32))
    )
    in_grad = jnp.take(returned, inverse_order, axis=1).swapaxes(0, 1).reshape(seq_len, half)

    out_weight_grad = core_join(side_join(*side_send(after(out_sum, two_sent), 1)))[:, 0].T
    qkv_grad = core_join(side_join(*side_send(qkv_sum, 3))).swapaxes(0, 1)

    packed = packed.reshape(ring_size, 2, 2, packed.shape[1])
    mine, sent = parts(packed, core, 2)
    packed = (mine + core_swap(sent))[:, :, 0]
    mine, sent = parts(packed, side, 1)
    packed = (mine + side_swap(sent))[:, 0]
    small_sum = take(packed, ring, 1, 0)
    for step in range(1, ring_size):
        sent = take(packed, (ring + step) % ring_size, 1, 0)
        small_sum = small_sum + ring_send(sent, step)
    small_sum = small_sum[0]
    vector_sum = small_sum[cut_two:]
    vector_sum = (vector_sum + lane_swap(vector_sum)).reshape(6, shard)
    return (
        outputs,
        in_grad,
        qkv_grad,
        small_sum[:cut_one].reshape(qv_bias.shape),
        out_weight_grad,
        vector_sum[0],
        vector_sum[1],
        vector_sum[2],
        up_weight_grad,
        small_sum[cut_one:cut_two].reshape(up_bias.shape),
        down_weight_grad,
        vector_sum[3],
        vector_sum[4],
        vector_sum[5],
    )


def solution(mesh):
    placed = (
        P("dp", "tensor"),
        P("dp", "tensor"),
        P(),
        P(),
        P(None, "dp", "tensor"),
        P(None, "tensor", "dp"),
        P("tensor", "dp"),
        P("dp"),
        P("dp"),
        P("dp"),
        P("dp", "tensor"),
        P("tensor", "dp"),
        P("tensor", "dp"),
        P("dp"),
        P("dp"),
        P("dp"),
    )
    return jax.shard_map(
        local,
        mesh=mesh,
        in_specs=placed,
        out_specs=(
            P("dp", "tensor"),
            P("dp", "tensor"),
            P(None, "dp", "tensor"),
            P(None, "tensor", "dp"),
            P("tensor", "dp"),
            P("dp"),
            P("dp"),
            P("dp"),
            P("dp", "tensor"),
            P("tensor", "dp"),
            P("tensor", "dp"),
            P("dp"),
            P("dp"),
            P("dp"),
        ),
        check_vma=False,
    )
```

```python
import functools
import math

import jax
import jax.numpy as jnp
from jax import lax
from jax.experimental import pallas as pl
from jax.experimental.pallas import tpu as pltpu
from jax.sharding import PartitionSpec as P

HD = 128


epsilon = 1e-05
neg_large = -1e30
low = jnp.bfloat16
wide = jnp.float32
COST_SCALE = 8


def norm_forward(hidden, gain, shift):
    center = hidden - jnp.mean(hidden, axis=-1, keepdims=True)
    inverse = lax.rsqrt(jnp.mean(center * center, axis=-1, keepdims=True) + epsilon)
    normed = center * inverse
    return (normed * gain + shift, normed, inverse)


def norm_backward(grad_rows, normed, inverse, gain):
    scaled = grad_rows * gain
    mean_first = jnp.mean(scaled, axis=-1, keepdims=True)
    mean_second = jnp.mean(scaled * normed, axis=-1, keepdims=True)
    result = inverse * (scaled - mean_first - normed * mean_second)
    return (result, jnp.sum(grad_rows * normed, axis=0), jnp.sum(grad_rows, axis=0))


def after(array, *others):
    return lax.optimization_barrier((array,) + others)[0] if others else array


def take(array, start, size, axis):
    return lax.dynamic_slice_in_dim(array, start, size, axis)


kernel_params = pltpu.CompilerParams(vmem_limit_bytes=40 * 1024 * 1024)


def product(left, right, left_axis, right_axis):
    dims = (((left_axis,), (right_axis,)), ((), ()))
    return lax.dot_general(left, right, dims, preferred_element_type=wide)


def call(kernel, flops, out_shape, **settings):
    return pl.pallas_call(
        kernel,
        out_shape=out_shape,
        compiler_params=kernel_params,
        cost_estimate=pl.CostEstimate(
            flops=flops // COST_SCALE, bytes_accessed=0, transcendentals=0
        ),
        **settings,
    )


def masked_probs(query, key, valid):
    scores = jnp.where(valid, product(query, key, 1, 1), neg_large)
    expo = jnp.exp((scores - jnp.max(scores, axis=-1, keepdims=True)) * HD ** (-0.5))
    return expo * (1.0 / jnp.sum(expo, axis=-1, keepdims=True))


def valid_keys(length, shift, rows):
    token = lax.broadcasted_iota(jnp.int32, (rows, rows), 1) + shift
    return jnp.where(token < rows, token, token - rows) < length


def attend_kernel(lengths, query, key, value, context):
    rows, features = query.shape
    valid = valid_keys(lengths[pl.program_id(0)], lengths[pl.num_programs(0)], rows)
    for head in range(features // HD):
        at = slice(head * HD, (head + 1) * HD)
        probs = masked_probs(query[:, at], key[:, at], valid)
        context[:, at] = product(probs.astype(low), value[:, at], 1, 0).astype(low)


def attend_back_kernel(lengths, query, key, value, grad, grads):
    rows, features = query.shape
    valid = valid_keys(lengths[pl.program_id(0)], lengths[pl.num_programs(0)], rows)
    for head in range(features // HD):
        at, key_at, value_at = (
            slice(c * features + head * HD, c * features + (head + 1) * HD) for c in range(3)
        )
        probs = masked_probs(query[:, at], key[:, at], valid)
        grads[:, value_at] = product(probs.astype(low), grad[:, at], 0, 0).astype(low)
        prob_grad = product(grad[:, at], value[:, at], 1, 1)
        mean = jnp.sum(prob_grad * probs, axis=-1, keepdims=True)
        score_grad = (probs * (prob_grad - mean)).astype(low)
        grads[:, at] = (product(score_grad, key[:, at], 1, 0) * HD ** (-0.5)).astype(low)
        grads[:, key_at] = (product(score_grad, query[:, at], 0, 0) * HD ** (-0.5)).astype(low)


def by_sequence(kernel, flops, seq_len, lengths, projected, *arrays):
    rows, columns = projected.shape
    features = columns // 3

    def spec(width, block):
        return pl.BlockSpec((seq_len, width), lambda sequence, lengths: (sequence, block))

    size = columns if arrays else features
    return call(
        kernel,
        flops,
        jax.ShapeDtypeStruct((rows, size), low),
        grid_spec=pltpu.PrefetchScalarGridSpec(
            num_scalar_prefetch=1,
            grid=(rows // seq_len,),
            in_specs=[spec(features, c) for c in range(3)] + [spec(features, 0) for a in arrays],
            out_specs=spec(size, 0),
        ),
    )(lengths, projected, projected, projected, *arrays)


def matmul_kernel(right_axis, left, right, *rest):
    total = product(left[...], right[...], 1, right_axis)
    if len(rest) == 2:
        total = total + rest[0][...]
    rest[-1][...] = total.astype(low)


def right_spec(depth, tile, right_axis, start):
    if right_axis:
        return pl.BlockSpec((tile, depth), lambda j: (j, start // depth))
    return pl.BlockSpec((depth, tile), lambda j: (0, start // tile + j))


def column_spec(rows, tile):
    return pl.BlockSpec((rows, tile), lambda j: (0, j))


def matmul(left, right, right_axis, size, start=0, bias=None):
    rows, depth = left.shape
    tile = math.gcd(size, 512 if right_axis or start % 512 == 0 else 256)
    in_specs = [
        pl.BlockSpec((rows, depth), lambda j: (0, 0)),
        right_spec(depth, tile, right_axis, start),
    ]
    operands = [left, right]
    if bias is not None:
        in_specs.append(column_spec(1, tile))
        operands.append(bias[None])
    return call(
        functools.partial(matmul_kernel, right_axis),
        2 * rows * depth * size,
        jax.ShapeDtypeStruct((rows, size), low),
        grid=(size // tile,),
        in_specs=in_specs,
        out_specs=column_spec(rows, tile),
    )(*operands)


def gelu_tanh(values):
    return jnp.tanh((2.0 / math.pi) ** 0.5 * (values + 0.044715 * values * values * values))


def gelu_slope(values):
    tanh = gelu_tanh(values)
    inner = (2.0 / math.pi) ** 0.5 * (1.0 + 3.0 * 0.044715 * values * values)
    return 0.5 * (1.0 + tanh) + 0.5 * values * (1.0 - tanh * tanh) * inner


def up_kernel(rows, weight, bias, pre_act, hidden):
    values = product(rows[...], weight[...], 1, 0) + bias[...]
    pre_act[...] = values
    hidden[...] = (0.5 * values * (1.0 + gelu_tanh(values))).astype(low)


def up_matmul(rows, weight, bias, tile=256):
    count, units = rows.shape[0], bias.shape[0]
    return call(
        up_kernel,
        2 * rows.size * units,
        [
            jax.ShapeDtypeStruct((count, units), wide),
            jax.ShapeDtypeStruct((count, units), low),
        ],
        grid=(units // tile,),
        in_specs=[
            pl.BlockSpec(rows.shape, lambda j: (0, 0)),
            right_spec(rows.shape[1], tile, 0, 0),
            column_spec(1, tile),
        ],
        out_specs=[column_spec(count, tile)] * 2,
    )(rows, weight, bias[None])


def up_back_kernel(grads, weight, slope, pre_grad, bias_grad):
    values = product(grads[...], weight[...], 1, 0) * slope[...].astype(wide)
    rounded = values.astype(low)
    pre_grad[...] = rounded
    bias_grad[...] = jnp.sum(rounded.astype(wide), axis=0, keepdims=True)


def up_back_matmul(grads, weight, slope, tile=256):
    count, units = slope.shape
    return call(
        up_back_kernel,
        2 * grads.size * units,
        [jax.ShapeDtypeStruct((count, units), low), jax.ShapeDtypeStruct((1, units), wide)],
        grid=(units // tile,),
        in_specs=[
            pl.BlockSpec(grads.shape, lambda j: (0, 0)),
            right_spec(grads.shape[1], tile, 0, weight.shape[1] - units),
            column_spec(count, tile),
        ],
        out_specs=[column_spec(count, tile), column_spec(1, tile)],
    )(grads, weight, slope)


def pair_kernel(left_one, right_one, left_two, right_two, total):
    one = product(left_one[...], right_one[...], 0, 0)
    total[...] = (one + product(left_two[...], right_two[...], 0, 0)).astype(low)


def pair_matmul(lefts, rights, tile=256):
    rows, depth = lefts[0].shape
    columns = rights[0].shape[1]
    specs = [column_spec(rows, tile), pl.BlockSpec((rows, columns), lambda j: (0, 0))]
    return call(
        pair_kernel,
        4 * rows * depth * columns,
        jax.ShapeDtypeStruct((depth, columns), low),
        grid=(depth // tile,),
        in_specs=specs * 2,
        out_specs=pl.BlockSpec((tile, columns), lambda j: (j, 0)),
    )(lefts[0], rights[0], lefts[1], rights[1])


def local(
    inputs,
    out_grad,
    lengths,
    dealing,
    qkv_weight,
    qv_bias,
    out_weight,
    out_bias,
    attn_gain,
    attn_shift,
    up_weight,
    up_bias,
    down_weight,
    down_bias,
    ffn_gain,
    ffn_shift,
):
    groups = lax.axis_size("dp")
    ring_size = groups // 4
    index = lax.axis_index("dp")
    core, side, ring = index % 2, (index // 2) % 2, index // 4
    lane = lax.axis_index("tensor")
    core_pairs = [(i, i ^ 1) for i in range(groups)]
    side_pairs = [(i, i ^ 2) for i in range(groups)]
    ring_groups = [[4 * r + offset for r in range(ring_size)] for offset in range(4)]

    def core_swap(array):
        return lax.ppermute(array, "dp", core_pairs)

    def side_swap(array):
        return lax.ppermute(array, "dp", side_pairs)

    def ring_send(array, steps):
        return lax.ppermute(array, "dp", [(i, (i + 4 * steps) % groups) for i in range(groups)])

    def lane_swap(array):
        return lax.ppermute(array, "tensor", [(0, 1), (1, 0)])

    def in_order(bit, mine, theirs, axis):
        first = jnp.where(bit == 0, mine, theirs)
        second = jnp.where(bit == 0, theirs, mine)
        return jnp.concatenate([first, second], axis=axis)

    def parts(array, bit, axis):
        size = array.shape[axis] // 2
        return take(array, bit * size, size, axis), take(array, (1 - bit) * size, size, axis)

    seq_len, half = inputs.shape
    width = 2 * half
    per_peer = seq_len // groups
    shard = width // groups
    token_half = seq_len // 2
    features = half // 4
    units = up_weight.shape[1] // 4

    def split_weight(weight):
        mine, sent = parts(weight, core, 2)
        weight = in_order(core, mine, core_swap(sent), 0)
        mine, sent = parts(weight, side, 2)
        weight = in_order(side, mine, side_swap(sent), 0)
        return weight.reshape(4 * shard, -1)

    def gather_weight(piece):
        return lax.all_gather(piece, "dp", axis=0, axis_index_groups=ring_groups, tiled=True)

    first_weights = jnp.concatenate([qkv_weight, out_weight.T[None]], axis=0).swapaxes(0, 1)
    first_piece = split_weight(first_weights)
    first_full = gather_weight(first_piece)

    small = jnp.concatenate(
        [
            v.reshape(-1)
            for v in (
                qv_bias,
                up_bias,
                out_bias,
                attn_gain,
                attn_shift,
                down_bias,
                ffn_gain,
                ffn_shift,
            )
        ]
    )[None]
    small = in_order(core, small, core_swap(after(small, first_piece)), 0)
    small = in_order(side, small, side_swap(small), 0)
    small_all = lax.dynamic_update_slice_in_dim(
        jnp.zeros((groups, small.shape[1]), low), small, ring * 4, 0
    )
    for step in range(1, ring_size):
        place = ((ring - step) % ring_size) * 4
        small_all = lax.dynamic_update_slice_in_dim(small_all, ring_send(small, step), place, 0)

    local_rows = inputs.reshape(groups, per_peer, half).swapaxes(0, 1)
    sending = jnp.take(local_rows, dealing, axis=1)
    arrived = lax.all_to_all(sending, "dp", split_axis=1, concat_axis=1, tiled=True)
    tokens = after(arrived, first_piece).reshape(seq_len, half)
    second_weights = after(up_weight, arrived), after(down_weight, arrived).T
    second_piece = split_weight(jnp.stack(second_weights, axis=1))
    second_full = gather_weight(second_piece)
    early, late = tokens[:token_half], tokens[token_half:]
    early = in_order(lane, early, lane_swap(early), 1)
    early = jnp.stack([early, side_swap(early)])
    late = jnp.stack([late, side_swap(late)])
    late = in_order(lane, late, lane_swap(late), 2)
    own_rows = jnp.stack([jnp.where(lane == 0, early, late), jnp.where(lane == 0, late, early)], 1)
    own_rows = after(own_rows.reshape(2 * seq_len, width), second_piece, small_all)
    all_rows = (own_rows, core_swap(own_rows))
    residual = own_rows[:token_half]
    grad_keep, grad_send = parts(out_grad, lane, 0)
    cotangent = in_order(lane, grad_keep, lane_swap(grad_send), 1)

    cut_one = qv_bias.size
    cut_two = cut_one + up_bias.size
    qv_full = (
        small_all[:, :cut_one]
        .reshape((groups,) + qv_bias.shape)
        .transpose(1, 2, 0, 3)
        .reshape(2, half)
    )
    up_bias_full = (
        small_all[:, cut_one:cut_two]
        .reshape((groups,) + up_bias.shape)
        .transpose(1, 0, 2)
        .reshape(-1)
    )
    vectors = (
        small_all[:, cut_two:].reshape(groups, 6, shard).transpose(1, 0, 2).reshape(6, width)
    ).astype(wide)
    out_bias_full, gain_one, shift_one, down_bias_full, gain_two, shift_two = vectors
    place = core * 2 + side
    qv_rows = take(qv_full, place * features, features, 1)
    up_bias_mine = take(up_bias_full, place * units, units, 0)

    def core_parts(left, right, start=0):
        theirs = core_swap(matmul(left[1], right, 1, width, start))
        mine = matmul(left[0], right, 1, width, start)
        return mine, theirs

    def added(both, pick):
        mine, theirs = (pick(array.reshape(2, 2, token_half, width)) for array in both)
        return mine.astype(wide) + theirs.astype(wide)

    def group_sum(both, beside_one=(), beside_two=()):
        one = side_swap(added(both, lambda a: a[1, ..., :half]).astype(low))
        two = lane_swap(added(both, lambda a: a[:, 1, :, half:]).astype(low))
        one = added(both, lambda a: a[0, ..., :half]) + after(one, *beside_one).astype(wide)
        two = added(both, lambda a: a[:, 0, :, half:]) + after(two, *beside_one).astype(wide)
        one = one[0] + after(lane_swap(one[1].astype(low)), *beside_two).astype(wide)
        two = two[0] + after(side_swap(two[1].astype(low)), *beside_two).astype(wide)
        return jnp.concatenate([one, two], axis=1)

    def group_gather(rows, beside_own=()):
        one, two = rows[:, :half], rows[:, half:]
        one = jnp.stack([one, lane_swap(one)])
        two = jnp.stack([two, side_swap(two)])
        one = jnp.stack([one, side_swap(one)])
        two = jnp.stack([two, lane_swap(two)], axis=1)
        own = jnp.concatenate([one, two], axis=3).reshape(2 * seq_len, width)
        own = after(own, *beside_own)
        return own, core_swap(own)

    sequences = jnp.stack([index, index ^ 2, index ^ 1, index ^ 3])
    group_lengths = jnp.take(lengths, jnp.take(dealing, sequences)).reshape(2, 2)
    group_lengths = jnp.concatenate(
        [group_lengths, jnp.full((2, 1), lane * token_half, jnp.int32)], axis=1
    )
    qkv_bias = jnp.concatenate([qv_rows[0], jnp.zeros_like(qv_rows[0]), qv_rows[1]]).astype(wide)
    flops = 4 * 2 * seq_len * seq_len * features
    projected, context = [], []
    for i in range(2):
        rows = after(all_rows[i], *context)
        projected.append(matmul(rows, first_full, 0, 3 * features, bias=qkv_bias))
        context.append(
            by_sequence(attend_kernel, 4 * flops, seq_len, group_lengths[i], projected[i])
        )
    attended = group_sum(core_parts(context, first_full, 3 * features)) + out_bias_full
    first, normed_one, inverse_one = norm_forward(
        residual.astype(wide) + attended, gain_one, shift_one
    )
    first_low = group_gather(first.astype(low), [second_full])

    pre_act, hidden = [], []
    for i in range(2):
        values, outs = up_matmul(after(first_low[i], *hidden), second_full, up_bias_mine.astype(wide))
        pre_act.append(values)
        hidden.append(outs)
    mixed_parts = core_parts(hidden, second_full, units)
    slope = [gelu_slope(after(values, *mixed_parts)).astype(low) for values in pre_act]
    mixed = group_sum(mixed_parts, slope) + down_bias_full
    final, normed_two, inverse_two = norm_forward(first + mixed, gain_two, shift_two)
    second_grad, gain_two_grad, shift_two_grad = norm_backward(
        cotangent.astype(wide), normed_two, inverse_two, gain_two
    )
    mixed_low = second_grad.astype(low)
    down_bias_grad = jnp.sum(mixed_low, axis=0, dtype=wide)
    mixed_grad = group_gather(mixed_low)

    def scatter(partial):
        return lax.psum_scatter(
            partial, "dp", scatter_dimension=0, axis_index_groups=ring_groups, tiled=True
        )

    def side_send(total, kinds):
        total = total.reshape(4 * shard, kinds, -1)
        mine, sent = parts(total, side, 0)
        return mine, side_swap(sent)

    def side_join(mine, theirs):
        return in_order(side, mine, theirs, 2)

    def core_join(total):
        mine, sent = parts(total, core, 0)
        return in_order(core, mine, core_swap(sent), 2).astype(wide)

    pre_grad = [up_back_matmul(mixed_grad[0], second_full, slope[0])]
    mixed_grad = (mixed_grad[0], after(mixed_grad[1], pre_grad[0][0]))
    down_partial = pair_matmul(mixed_grad, hidden)
    down_sum = scatter(down_partial)
    pre_grad.append(up_back_matmul(after(mixed_grad[1], down_partial), second_full, slope[1]))
    pre_grad, up_bias_grad = zip(*pre_grad, strict=True)
    both = core_parts(pre_grad, second_full)
    up_partial = pair_matmul(first_low, [after(grads, *both) for grads in pre_grad])
    up_sum = scatter(up_partial)
    first_grad = second_grad + group_sum(both, [up_partial], [down_sum])
    attn_total_grad, gain_one_grad, shift_one_grad = norm_backward(
        first_grad, normed_one, inverse_one, gain_one
    )
    attended_low = attn_total_grad.astype(low)
    out_bias_grad = jnp.sum(attended_low, axis=0, dtype=wide)
    attended_grad = group_gather(attended_low)
    down_sum = side_send(down_sum, 1)
    stacked, parts_grad = [], []
    for i in range(2):
        rows = after(attended_grad[i], *parts_grad)
        if i:
            rows = after(rows, down_sum[1])
        context_grad = matmul(rows, first_full, 0, features, 3 * features)
        stacked.append(
            by_sequence(
                attend_back_kernel,
                8 * flops,
                seq_len,
                group_lengths[i],
                projected[i],
                context_grad,
            )
        )
        parts_grad.append(matmul(stacked[i], first_full, 1, width))
    mine, theirs = parts_grad
    qkv_partial = pair_matmul(all_rows, [after(grads, theirs) for grads in stacked])
    qkv_sum = scatter(qkv_partial)
    theirs = core_swap(theirs)
    up_sum = side_send(up_sum, 1)
    out_partial = pair_matmul(attended_grad, [after(rows, qkv_partial) for rows in context])
    out_sum = scatter(out_partial)
    theirs = after(theirs, out_partial, up_sum[1])
    quarter = half // 2
    both = tuple(array.reshape(2, seq_len, width) for array in (after(mine, up_sum[1]), theirs))

    def summed(pick):
        return sum(pick(array).astype(wide) for array in both)

    def across(array):
        return jnp.concatenate([array[..., :quarter], array[..., half : half + quarter]], axis=-1)

    def of_lane(bit):
        return lambda array: take(array, bit * half + quarter, quarter, 2)

    def lane_swap_rows(array):
        array = lane_swap(array)
        return jnp.concatenate([array[..., token_half:, :], array[..., :token_half, :]], axis=-2)

    one_sent = summed(lambda array: across(array[1])).astype(low)
    two_sent = summed(of_lane(1 - lane)).astype(low)
    one, two = side_swap(one_sent), lane_swap_rows(two_sent)
    one = summed(lambda array: across(array[0])) + one.astype(wide)
    two = summed(of_lane(lane)) + two.astype(wide)
    one_sent = take(one, (1 - lane) * quarter, quarter, 1).astype(low)
    two_sent = two[1].astype(low)
    down_weight_grad = core_join(after(side_join(*down_sum), one_sent))[:, 0].T
    up_weight_grad = core_join(after(side_join(*up_sum), one_sent))[:, 0]
    one_theirs = after(lane_swap(one_sent), down_weight_grad, up_weight_grad)
    one_theirs = jnp.concatenate([one_theirs[token_half:], one_theirs[:token_half]], axis=0)
    one = take(one, lane * quarter, quarter, 1) + one_theirs.astype(wide)
    two = two[0] + side_swap(two_sent).astype(wide)
    own_attended = take(attended_grad[0][:seq_len], lane * half, half, 1)
    in_half = (jnp.concatenate([one, two], axis=1) + own_attended.astype(wide)).astype(low)
    in_half = in_order(lane, in_half[:token_half], in_half[token_half:], 0)
    back_rows = after(in_half, qkv_sum).reshape(per_peer, groups, half)
    out_keep, out_send = parts(final.astype(low), lane, 1)
    outputs = in_order(lane, out_keep, lane_swap(after(out_send, qkv_sum)), 0)
    qkv_bias_sum = sum(jnp.sum(after(s, two_sent), axis=0, dtype=wide) for s in stacked)
    qkv_bias_sum = qkv_bias_sum.reshape(3, features)
    qv_grad = jnp.stack([qkv_bias_sum[0], qkv_bias_sum[2]])
    def spread(mine, size):
        full = jnp.zeros(mine.shape[:-1] + (4 * size,), wide)
        return lax.dynamic_update_slice_in_dim(full, mine, place * size, mine.ndim - 1)

    qv_spread = (
        spread(qv_grad, features)
        .reshape(2, qv_bias.shape[1], groups, qv_bias.shape[2])
        .transpose(2, 0, 1, 3)
        .reshape(groups, -1)
    )
    up_spread = (
        spread((up_bias_grad[0] + up_bias_grad[1])[0], units)
        .reshape(up_bias.shape[0], groups, up_bias.shape[1])
        .transpose(1, 0, 2)
        .reshape(groups, -1)
    )
    vector_spread = (
        jnp.stack(
            [
                out_bias_grad,
                gain_one_grad,
                shift_one_grad,
                down_bias_grad,
                gain_two_grad,
                shift_two_grad,
            ]
        )
        .reshape(6, groups, shard)
        .transpose(1, 0, 2)
        .reshape(groups, -1)
    )
    packed = jnp.concatenate([qv_spread, up_spread, vector_spread], axis=1)
    packed = after(packed, qkv_sum)

    returned = lax.all_to_all(back_rows, "dp", split_axis=1, concat_axis=1, tiled=True)
    inverse_order = (
        jnp.zeros((groups,), jnp.int32).at[dealing].set(jnp.arange(groups, dtype=jnp.int32))
    )
    in_grad = jnp.take(returned, inverse_order, axis=1).swapaxes(0, 1).reshape(seq_len, half)

    out_weight_grad = core_join(side_join(*side_send(after(out_sum, qkv_sum), 1)))[:, 0].T
    qkv_grad = core_join(side_join(*side_send(qkv_sum, 3))).swapaxes(0, 1)

    packed = packed.reshape(ring_size, 2, 2, packed.shape[1])
    mine, sent = parts(packed, core, 2)
    packed = (mine + core_swap(sent))[:, :, 0]
    mine, sent = parts(packed, side, 1)
    packed = (mine + side_swap(sent))[:, 0]
    small_sum = take(packed, ring, 1, 0)
    for step in range(1, ring_size):
        sent = take(packed, (ring + step) % ring_size, 1, 0)
        small_sum = small_sum + ring_send(sent, step)
    small_sum = small_sum[0]
    vector_sum = small_sum[cut_two:]
    vector_sum = (vector_sum + lane_swap(vector_sum)).reshape(6, shard)
    return (
        outputs,
        in_grad,
        qkv_grad,
        small_sum[:cut_one].reshape(qv_bias.shape),
        out_weight_grad,
        vector_sum[0],
        vector_sum[1],
        vector_sum[2],
        up_weight_grad,
        small_sum[cut_one:cut_two].reshape(up_bias.shape),
        down_weight_grad,
        vector_sum[3],
        vector_sum[4],
        vector_sum[5],
    )


def solution(mesh):
    placed = (
        P("dp", "tensor"),
        P("dp", "tensor"),
        P(),
        P(),
        P(None, "dp", "tensor"),
        P(None, "tensor", "dp"),
        P("tensor", "dp"),
        P("dp"),
        P("dp"),
        P("dp"),
        P("dp", "tensor"),
        P("tensor", "dp"),
        P("tensor", "dp"),
        P("dp"),
        P("dp"),
        P("dp"),
    )
    return jax.shard_map(
        local,
        mesh=mesh,
        in_specs=placed,
        out_specs=(
            P("dp", "tensor"),
            P("dp", "tensor"),
            P(None, "dp", "tensor"),
            P(None, "tensor", "dp"),
            P("tensor", "dp"),
            P("dp"),
            P("dp"),
            P("dp"),
            P("dp", "tensor"),
            P("tensor", "dp"),
            P("tensor", "dp"),
            P("dp"),
            P("dp"),
            P("dp"),
        ),
        check_vma=False,
    )
```

```python
import functools
import math

import jax
import jax.numpy as jnp
from jax import lax
from jax.experimental import pallas as pl
from jax.experimental.pallas import tpu as pltpu
from jax.sharding import PartitionSpec as P

HD = 128


epsilon = 1e-05
neg_large = -1e30
low = jnp.bfloat16
wide = jnp.float32
COST_SCALE = 8


def norm_forward(hidden, gain, shift):
    center = hidden - jnp.mean(hidden, axis=-1, keepdims=True)
    inverse = lax.rsqrt(jnp.mean(center * center, axis=-1, keepdims=True) + epsilon)
    normed = center * inverse
    return (normed * gain + shift, normed, inverse)


def norm_backward(grad_rows, normed, inverse, gain):
    scaled = grad_rows * gain
    mean_first = jnp.mean(scaled, axis=-1, keepdims=True)
    mean_second = jnp.mean(scaled * normed, axis=-1, keepdims=True)
    result = inverse * (scaled - mean_first - normed * mean_second)
    return (result, jnp.sum(grad_rows * normed, axis=0), jnp.sum(grad_rows, axis=0))


def after(array, *others):
    return lax.optimization_barrier((array,) + others)[0] if others else array


def take(array, start, size, axis):
    return lax.dynamic_slice_in_dim(array, start, size, axis)


kernel_params = pltpu.CompilerParams(vmem_limit_bytes=40 * 1024 * 1024)


def product(left, right, left_axis, right_axis):
    dims = (((left_axis,), (right_axis,)), ((), ()))
    return lax.dot_general(left, right, dims, preferred_element_type=wide)


def call(kernel, flops, out_shape, **settings):
    return pl.pallas_call(
        kernel,
        out_shape=out_shape,
        compiler_params=kernel_params,
        cost_estimate=pl.CostEstimate(
            flops=flops // COST_SCALE, bytes_accessed=0, transcendentals=0
        ),
        **settings,
    )


def masked_probs(query, key, valid):
    scores = jnp.where(valid, product(query, key, 1, 1), neg_large)
    expo = jnp.exp((scores - jnp.max(scores, axis=-1, keepdims=True)) * HD ** (-0.5))
    return expo * (1.0 / jnp.sum(expo, axis=-1, keepdims=True))


def valid_keys(length, shift, rows):
    token = lax.broadcasted_iota(jnp.int32, (rows, rows), 1) + shift
    return jnp.where(token < rows, token, token - rows) < length


def attend_kernel(lengths, query, key, value, context):
    rows, features = query.shape
    valid = valid_keys(lengths[pl.program_id(0)], lengths[pl.num_programs(0)], rows)
    for head in range(features // HD):
        at = slice(head * HD, (head + 1) * HD)
        probs = masked_probs(query[:, at], key[:, at], valid)
        context[:, at] = product(probs.astype(low), value[:, at], 1, 0).astype(low)


def attend_back_kernel(lengths, query, key, value, grad, grads):
    rows, features = query.shape
    valid = valid_keys(lengths[pl.program_id(0)], lengths[pl.num_programs(0)], rows)
    for head in range(features // HD):
        at, key_at, value_at = (
            slice(c * features + head * HD, c * features + (head + 1) * HD) for c in range(3)
        )
        probs = masked_probs(query[:, at], key[:, at], valid)
        grads[:, value_at] = product(probs.astype(low), grad[:, at], 0, 0).astype(low)
        prob_grad = product(grad[:, at], value[:, at], 1, 1)
        mean = jnp.sum(prob_grad * probs, axis=-1, keepdims=True)
        score_grad = (probs * (prob_grad - mean)).astype(low)
        grads[:, at] = (product(score_grad, key[:, at], 1, 0) * HD ** (-0.5)).astype(low)
        grads[:, key_at] = (product(score_grad, query[:, at], 0, 0) * HD ** (-0.5)).astype(low)


def by_sequence(kernel, flops, seq_len, lengths, projected, *arrays):
    rows, columns = projected.shape
    features = columns // 3

    def spec(width, block):
        return pl.BlockSpec((seq_len, width), lambda sequence, lengths: (sequence, block))

    size = columns if arrays else features
    return call(
        kernel,
        flops,
        jax.ShapeDtypeStruct((rows, size), low),
        grid_spec=pltpu.PrefetchScalarGridSpec(
            num_scalar_prefetch=1,
            grid=(rows // seq_len,),
            in_specs=[spec(features, c) for c in range(3)] + [spec(features, 0) for a in arrays],
            out_specs=spec(size, 0),
        ),
    )(lengths, projected, projected, projected, *arrays)


def matmul_kernel(right_axis, left, right, *rest):
    total = product(left[...], right[...], 1, right_axis)
    if len(rest) == 2:
        total = total + rest[0][...]
    rest[-1][...] = total.astype(low)


def right_spec(depth, tile, right_axis, start):
    if right_axis:
        return pl.BlockSpec((tile, depth), lambda j: (j, start // depth))
    return pl.BlockSpec((depth, tile), lambda j: (0, start // tile + j))


def column_spec(rows, tile):
    return pl.BlockSpec((rows, tile), lambda j: (0, j))


def matmul(left, right, right_axis, size, start=0, bias=None):
    rows, depth = left.shape
    tile = math.gcd(size, 512 if right_axis or start % 512 == 0 else 256)
    in_specs = [
        pl.BlockSpec((rows, depth), lambda j: (0, 0)),
        right_spec(depth, tile, right_axis, start),
    ]
    operands = [left, right]
    if bias is not None:
        in_specs.append(column_spec(1, tile))
        operands.append(bias[None])
    return call(
        functools.partial(matmul_kernel, right_axis),
        2 * rows * depth * size,
        jax.ShapeDtypeStruct((rows, size), low),
        grid=(size // tile,),
        in_specs=in_specs,
        out_specs=column_spec(rows, tile),
    )(*operands)


def gelu_tanh(values):
    return jnp.tanh((2.0 / math.pi) ** 0.5 * (values + 0.044715 * values * values * values))


def gelu_slope(values):
    tanh = gelu_tanh(values)
    inner = (2.0 / math.pi) ** 0.5 * (1.0 + 3.0 * 0.044715 * values * values)
    return 0.5 * (1.0 + tanh) + 0.5 * values * (1.0 - tanh * tanh) * inner


def up_kernel(rows, weight, bias, pre_act, hidden):
    values = product(rows[...], weight[...], 1, 0) + bias[...]
    pre_act[...] = values
    hidden[...] = (0.5 * values * (1.0 + gelu_tanh(values))).astype(low)


def up_matmul(rows, weight, bias, tile=256):
    count, units = rows.shape[0], bias.shape[0]
    return call(
        up_kernel,
        2 * rows.size * units,
        [
            jax.ShapeDtypeStruct((count, units), wide),
            jax.ShapeDtypeStruct((count, units), low),
        ],
        grid=(units // tile,),
        in_specs=[
            pl.BlockSpec(rows.shape, lambda j: (0, 0)),
            right_spec(rows.shape[1], tile, 0, 0),
            column_spec(1, tile),
        ],
        out_specs=[column_spec(count, tile)] * 2,
    )(rows, weight, bias[None])


def up_back_kernel(grads, weight, slope, pre_grad, bias_grad):
    values = product(grads[...], weight[...], 1, 0) * slope[...].astype(wide)
    rounded = values.astype(low)
    pre_grad[...] = rounded
    bias_grad[...] = jnp.sum(rounded.astype(wide), axis=0, keepdims=True)


def up_back_matmul(grads, weight, slope, tile=256):
    count, units = slope.shape
    return call(
        up_back_kernel,
        2 * grads.size * units,
        [jax.ShapeDtypeStruct((count, units), low), jax.ShapeDtypeStruct((1, units), wide)],
        grid=(units // tile,),
        in_specs=[
            pl.BlockSpec(grads.shape, lambda j: (0, 0)),
            right_spec(grads.shape[1], tile, 0, weight.shape[1] - units),
            column_spec(count, tile),
        ],
        out_specs=[column_spec(count, tile), column_spec(1, tile)],
    )(grads, weight, slope)


def pair_kernel(left_one, right_one, left_two, right_two, total):
    one = product(left_one[...], right_one[...], 0, 0)
    total[...] = (one + product(left_two[...], right_two[...], 0, 0)).astype(low)


def pair_matmul(lefts, rights, tile=256):
    rows, depth = lefts[0].shape
    columns = rights[0].shape[1]
    specs = [column_spec(rows, tile), pl.BlockSpec((rows, columns), lambda j: (0, 0))]
    return call(
        pair_kernel,
        4 * rows * depth * columns,
        jax.ShapeDtypeStruct((depth, columns), low),
        grid=(depth // tile,),
        in_specs=specs * 2,
        out_specs=pl.BlockSpec((tile, columns), lambda j: (j, 0)),
    )(lefts[0], rights[0], lefts[1], rights[1])


def local(
    inputs,
    out_grad,
    lengths,
    dealing,
    qkv_weight,
    qv_bias,
    out_weight,
    out_bias,
    attn_gain,
    attn_shift,
    up_weight,
    up_bias,
    down_weight,
    down_bias,
    ffn_gain,
    ffn_shift,
):
    groups = lax.axis_size("dp")
    ring_size = groups // 4
    index = lax.axis_index("dp")
    core, side, ring = index % 2, (index // 2) % 2, index // 4
    lane = lax.axis_index("tensor")
    core_pairs = [(i, i ^ 1) for i in range(groups)]
    side_pairs = [(i, i ^ 2) for i in range(groups)]
    ring_groups = [[4 * r + offset for r in range(ring_size)] for offset in range(4)]

    def core_swap(array):
        return lax.ppermute(array, "dp", core_pairs)

    def side_swap(array):
        return lax.ppermute(array, "dp", side_pairs)

    def ring_send(array, steps):
        return lax.ppermute(array, "dp", [(i, (i + 4 * steps) % groups) for i in range(groups)])

    def lane_swap(array):
        return lax.ppermute(array, "tensor", [(0, 1), (1, 0)])

    def in_order(bit, mine, theirs, axis):
        first = jnp.where(bit == 0, mine, theirs)
        second = jnp.where(bit == 0, theirs, mine)
        return jnp.concatenate([first, second], axis=axis)

    def parts(array, bit, axis):
        size = array.shape[axis] // 2
        return take(array, bit * size, size, axis), take(array, (1 - bit) * size, size, axis)

    seq_len, half = inputs.shape
    width = 2 * half
    per_peer = seq_len // groups
    shard = width // groups
    token_half = seq_len // 2
    features = half // 4
    units = up_weight.shape[1] // 4

    def split_weight(weight):
        mine, sent = parts(weight, core, 2)
        weight = in_order(core, mine, core_swap(sent), 0)
        mine, sent = parts(weight, side, 2)
        weight = in_order(side, mine, side_swap(sent), 0)
        return weight.reshape(4 * shard, -1)

    def gather_weight(piece):
        return lax.all_gather(piece, "dp", axis=0, axis_index_groups=ring_groups, tiled=True)

    first_weights = jnp.concatenate([qkv_weight, out_weight.T[None]], axis=0).swapaxes(0, 1)
    first_piece = split_weight(first_weights)
    first_full = gather_weight(first_piece)

    small = jnp.concatenate(
        [
            v.reshape(-1)
            for v in (
                qv_bias,
                up_bias,
                out_bias,
                attn_gain,
                attn_shift,
                down_bias,
                ffn_gain,
                ffn_shift,
            )
        ]
    )[None]
    small = in_order(core, small, core_swap(after(small, first_piece)), 0)
    small = in_order(side, small, side_swap(small), 0)
    small_all = lax.dynamic_update_slice_in_dim(
        jnp.zeros((groups, small.shape[1]), low), small, ring * 4, 0
    )
    for step in range(1, ring_size):
        place = ((ring - step) % ring_size) * 4
        small_all = lax.dynamic_update_slice_in_dim(small_all, ring_send(small, step), place, 0)

    local_rows = inputs.reshape(groups, per_peer, half).swapaxes(0, 1)
    sending = jnp.take(local_rows, dealing, axis=1)
    arrived = lax.all_to_all(sending, "dp", split_axis=1, concat_axis=1, tiled=True)
    tokens = after(arrived, first_piece).reshape(seq_len, half)
    second_weights = after(up_weight, arrived), after(down_weight, arrived).T
    second_piece = split_weight(jnp.stack(second_weights, axis=1))
    second_full = gather_weight(second_piece)
    early, late = tokens[:token_half], tokens[token_half:]
    early = in_order(lane, early, lane_swap(early), 1)
    early = jnp.stack([early, side_swap(early)])
    late = jnp.stack([late, side_swap(late)])
    late = in_order(lane, late, lane_swap(late), 2)
    own_rows = jnp.stack([jnp.where(lane == 0, early, late), jnp.where(lane == 0, late, early)], 1)
    own_rows = after(own_rows.reshape(2 * seq_len, width), second_piece, small_all)
    all_rows = (own_rows, core_swap(own_rows))
    residual = own_rows[:token_half]
    grad_keep, grad_send = parts(out_grad, lane, 0)
    cotangent = in_order(lane, grad_keep, lane_swap(grad_send), 1)

    cut_one = qv_bias.size
    cut_two = cut_one + up_bias.size
    qv_full = (
        small_all[:, :cut_one]
        .reshape((groups,) + qv_bias.shape)
        .transpose(1, 2, 0, 3)
        .reshape(2, half)
    )
    up_bias_full = (
        small_all[:, cut_one:cut_two]
        .reshape((groups,) + up_bias.shape)
        .transpose(1, 0, 2)
        .reshape(-1)
    )
    vectors = (
        small_all[:, cut_two:].reshape(groups, 6, shard).transpose(1, 0, 2).reshape(6, width)
    ).astype(wide)
    out_bias_full, gain_one, shift_one, down_bias_full, gain_two, shift_two = vectors
    place = core * 2 + side
    qv_rows = take(qv_full, place * features, features, 1)
    up_bias_mine = take(up_bias_full, place * units, units, 0)

    def core_parts(left, right, start=0):
        theirs = core_swap(matmul(left[1], right, 1, width, start))
        mine = matmul(left[0], right, 1, width, start)
        return mine, theirs

    def added(both, pick):
        mine, theirs = (pick(array.reshape(2, 2, token_half, width)) for array in both)
        return mine.astype(wide) + theirs.astype(wide)

    def group_sum(both, beside_one=(), beside_two=()):
        one = side_swap(added(both, lambda a: a[1, ..., :half]).astype(low))
        two = lane_swap(added(both, lambda a: a[:, 1, :, half:]).astype(low))
        one = added(both, lambda a: a[0, ..., :half]) + after(one, *beside_one).astype(wide)
        two = added(both, lambda a: a[:, 0, :, half:]) + after(two, *beside_one).astype(wide)
        one = one[0] + after(lane_swap(one[1].astype(low)), *beside_two).astype(wide)
        two = two[0] + after(side_swap(two[1].astype(low)), *beside_two).astype(wide)
        return jnp.concatenate([one, two], axis=1)

    def group_gather(rows, beside_own=()):
        one, two = rows[:, :half], rows[:, half:]
        one = jnp.stack([one, lane_swap(one)])
        two = jnp.stack([two, side_swap(two)])
        one = jnp.stack([one, side_swap(one)])
        two = jnp.stack([two, lane_swap(two)], axis=1)
        own = jnp.concatenate([one, two], axis=3).reshape(2 * seq_len, width)
        own = after(own, *beside_own)
        return own, core_swap(own)

    sequences = jnp.stack([index, index ^ 2, index ^ 1, index ^ 3])
    group_lengths = jnp.take(lengths, jnp.take(dealing, sequences)).reshape(2, 2)
    group_lengths = jnp.concatenate(
        [group_lengths, jnp.full((2, 1), lane * token_half, jnp.int32)], axis=1
    )
    qkv_bias = jnp.concatenate([qv_rows[0], jnp.zeros_like(qv_rows[0]), qv_rows[1]]).astype(wide)
    flops = 4 * 2 * seq_len * seq_len * features
    projected, context = [], []
    for i in range(2):
        rows = after(all_rows[i], *context)
        projected.append(matmul(rows, first_full, 0, 3 * features, bias=qkv_bias))
        context.append(
            by_sequence(attend_kernel, 4 * flops, seq_len, group_lengths[i], projected[i])
        )
    attended = group_sum(core_parts(context, first_full, 3 * features)) + out_bias_full
    first, normed_one, inverse_one = norm_forward(
        residual.astype(wide) + attended, gain_one, shift_one
    )
    first_low = group_gather(first.astype(low), [second_full])

    pre_act, hidden = [], []
    for i in range(2):
        values, outs = up_matmul(after(first_low[i], *hidden), second_full, up_bias_mine.astype(wide))
        pre_act.append(values)
        hidden.append(outs)
    mixed_parts = core_parts(hidden, second_full, units)
    slope = [gelu_slope(after(values, *mixed_parts)).astype(low) for values in pre_act]
    mixed = group_sum(mixed_parts, slope) + down_bias_full
    final, normed_two, inverse_two = norm_forward(first + mixed, gain_two, shift_two)
    second_grad, gain_two_grad, shift_two_grad = norm_backward(
        cotangent.astype(wide), normed_two, inverse_two, gain_two
    )
    mixed_low = second_grad.astype(low)
    down_bias_grad = jnp.sum(mixed_low, axis=0, dtype=wide)
    mixed_grad = group_gather(mixed_low)

    def scatter(partial):
        return lax.psum_scatter(
            partial, "dp", scatter_dimension=0, axis_index_groups=ring_groups, tiled=True
        )

    def side_send(total, kinds):
        total = total.reshape(4 * shard, kinds, -1)
        mine, sent = parts(total, side, 0)
        return mine, side_swap(sent)

    def side_join(mine, theirs):
        return in_order(side, mine, theirs, 2)

    def core_join(total):
        mine, sent = parts(total, core, 0)
        return in_order(core, mine, core_swap(sent), 2).astype(wide)

    pre_grad = [up_back_matmul(mixed_grad[0], second_full, slope[0])]
    mixed_grad = (mixed_grad[0], after(mixed_grad[1], pre_grad[0][0]))
    down_partial = pair_matmul(mixed_grad, hidden)
    down_sum = scatter(down_partial)
    pre_grad.append(up_back_matmul(after(mixed_grad[1], down_partial), second_full, slope[1]))
    pre_grad, up_bias_grad = zip(*pre_grad, strict=True)
    both = core_parts(pre_grad, second_full)
    up_partial = pair_matmul(first_low, [after(grads, *both) for grads in pre_grad])
    up_sum = scatter(up_partial)
    first_grad = second_grad + group_sum(both, [up_partial], [down_sum])
    attn_total_grad, gain_one_grad, shift_one_grad = norm_backward(
        first_grad, normed_one, inverse_one, gain_one
    )
    attended_low = attn_total_grad.astype(low)
    out_bias_grad = jnp.sum(attended_low, axis=0, dtype=wide)
    attended_grad = group_gather(attended_low)
    down_sum = side_send(down_sum, 1)
    stacked, parts_grad = [], []
    for i in range(2):
        rows = after(attended_grad[i], *parts_grad)
        if i:
            rows = after(rows, down_sum[1])
        context_grad = matmul(rows, first_full, 0, features, 3 * features)
        stacked.append(
            by_sequence(
                attend_back_kernel,
                8 * flops,
                seq_len,
                group_lengths[i],
                projected[i],
                context_grad,
            )
        )
        parts_grad.append(matmul(stacked[i], first_full, 1, width))
    mine, theirs = parts_grad
    qkv_partial = pair_matmul(all_rows, [after(grads, theirs) for grads in stacked])
    qkv_sum = scatter(qkv_partial)
    theirs = core_swap(theirs)
    theirs = after(theirs, up_sum)

    quarter = half // 2
    both = tuple(array.reshape(2, seq_len, width) for array in (after(mine, up_sum[1]), theirs))

    def summed(pick):
        return sum(pick(array).astype(wide) for array in both)

    def across(array):
        return jnp.concatenate([array[..., :quarter], array[..., half : half + quarter]], axis=-1)

    def of_lane(bit):
        return lambda array: take(array, bit * half + quarter, quarter, 2)

    def lane_swap_rows(array):
        array = lane_swap(array)
        return jnp.concatenate([array[..., token_half:, :], array[..., :token_half, :]], axis=-2)

    one_sent = summed(lambda array: across(array[1])).astype(low)
    two_sent = summed(of_lane(1 - lane)).astype(low)
    one, two = side_swap(one_sent), lane_swap_rows(two_sent)
    out_partial = pair_matmul(attended_grad, [after(rows, one_sent, two_sent) for rows in context])
    out_sum = scatter(out_partial)
    one = summed(lambda array: across(array[0])) + one.astype(wide)
    two = summed(of_lane(lane)) + two.astype(wide)
    one_sent = take(one, (1 - lane) * quarter, quarter, 1).astype(low)
    two_sent = two[1].astype(low)
    down_weight_grad = core_join(after(side_join(*down_sum), one_sent))[:, 0].T
    one_theirs = after(lane_swap(one_sent), down_weight_grad, out_partial)
    one_theirs = jnp.concatenate([one_theirs[token_half:], one_theirs[:token_half]], axis=0)
    one = take(one, lane * quarter, quarter, 1) + one_theirs.astype(wide)
    two = two[0] + side_swap(two_sent).astype(wide)
    own_attended = take(attended_grad[0][:seq_len], lane * half, half, 1)
    in_half = (jnp.concatenate([one, two], axis=1) + own_attended.astype(wide)).astype(low)
    in_half = in_order(lane, in_half[:token_half], in_half[token_half:], 0)
    back_rows = after(in_half, qkv_sum).reshape(per_peer, groups, half)
    out_keep, out_send = parts(final.astype(low), lane, 1)
    outputs = in_order(lane, out_keep, lane_swap(after(out_send, qkv_sum)), 0)
    qkv_bias_sum = sum(jnp.sum(after(s, two_sent), axis=0, dtype=wide) for s in stacked)
    qkv_bias_sum = qkv_bias_sum.reshape(3, features)
    qv_grad = jnp.stack([qkv_bias_sum[0], qkv_bias_sum[2]])
    def spread(mine, size):
        full = jnp.zeros(mine.shape[:-1] + (4 * size,), wide)
        return lax.dynamic_update_slice_in_dim(full, mine, place * size, mine.ndim - 1)

    qv_spread = (
        spread(qv_grad, features)
        .reshape(2, qv_bias.shape[1], groups, qv_bias.shape[2])
        .transpose(2, 0, 1, 3)
        .reshape(groups, -1)
    )
    up_spread = (
        spread((up_bias_grad[0] + up_bias_grad[1])[0], units)
        .reshape(up_bias.shape[0], groups, up_bias.shape[1])
        .transpose(1, 0, 2)
        .reshape(groups, -1)
    )
    vector_spread = (
        jnp.stack(
            [
                out_bias_grad,
                gain_one_grad,
                shift_one_grad,
                down_bias_grad,
                gain_two_grad,
                shift_two_grad,
            ]
        )
        .reshape(6, groups, shard)
        .transpose(1, 0, 2)
        .reshape(groups, -1)
    )
    packed = jnp.concatenate([qv_spread, up_spread, vector_spread], axis=1)
    packed = after(packed, qkv_sum)

    up_weight_grad = core_join(side_join(*side_send(after(up_sum, two_sent), 1)))[:, 0]
    returned = lax.all_to_all(back_rows, "dp", split_axis=1, concat_axis=1, tiled=True)
    inverse_order = (
        jnp.zeros((groups,), jnp.int32).at[dealing].set(jnp.arange(groups, dtype=jnp.int32))
    )
    in_grad = jnp.take(returned, inverse_order, axis=1).swapaxes(0, 1).reshape(seq_len, half)

    out_weight_grad = core_join(side_join(*side_send(after(out_sum, qkv_sum), 1)))[:, 0].T
    qkv_grad = core_join(side_join(*side_send(qkv_sum, 3))).swapaxes(0, 1)

    packed = packed.reshape(ring_size, 2, 2, packed.shape[1])
    mine, sent = parts(packed, core, 2)
    packed = (mine + core_swap(sent))[:, :, 0]
    mine, sent = parts(packed, side, 1)
    packed = (mine + side_swap(sent))[:, 0]
    small_sum = take(packed, ring, 1, 0)
    for step in range(1, ring_size):
        sent = take(packed, (ring + step) % ring_size, 1, 0)
        small_sum = small_sum + ring_send(sent, step)
    small_sum = small_sum[0]
    vector_sum = small_sum[cut_two:]
    vector_sum = (vector_sum + lane_swap(vector_sum)).reshape(6, shard)
    return (
        outputs,
        in_grad,
        qkv_grad,
        small_sum[:cut_one].reshape(qv_bias.shape),
        out_weight_grad,
        vector_sum[0],
        vector_sum[1],
        vector_sum[2],
        up_weight_grad,
        small_sum[cut_one:cut_two].reshape(up_bias.shape),
        down_weight_grad,
        vector_sum[3],
        vector_sum[4],
        vector_sum[5],
    )


def solution(mesh):
    placed = (
        P("dp", "tensor"),
        P("dp", "tensor"),
        P(),
        P(),
        P(None, "dp", "tensor"),
        P(None, "tensor", "dp"),
        P("tensor", "dp"),
        P("dp"),
        P("dp"),
        P("dp"),
        P("dp", "tensor"),
        P("tensor", "dp"),
        P("tensor", "dp"),
        P("dp"),
        P("dp"),
        P("dp"),
    )
    return jax.shard_map(
        local,
        mesh=mesh,
        in_specs=placed,
        out_specs=(
            P("dp", "tensor"),
            P("dp", "tensor"),
            P(None, "dp", "tensor"),
            P(None, "tensor", "dp"),
            P("tensor", "dp"),
            P("dp"),
            P("dp"),
            P("dp"),
            P("dp", "tensor"),
            P("tensor", "dp"),
            P("tensor", "dp"),
            P("dp"),
            P("dp"),
            P("dp"),
        ),
        check_vma=False,
    )
```

```python
import functools
import math

import jax
import jax.numpy as jnp
from jax import lax
from jax.experimental import pallas as pl
from jax.experimental.pallas import tpu as pltpu
from jax.sharding import PartitionSpec as P

HD = 128


epsilon = 1e-05
neg_large = -1e30
low = jnp.bfloat16
wide = jnp.float32
COST_SCALE = 8


def norm_forward(hidden, gain, shift):
    center = hidden - jnp.mean(hidden, axis=-1, keepdims=True)
    inverse = lax.rsqrt(jnp.mean(center * center, axis=-1, keepdims=True) + epsilon)
    normed = center * inverse
    return (normed * gain + shift, normed, inverse)


def norm_backward(grad_rows, normed, inverse, gain):
    scaled = grad_rows * gain
    mean_first = jnp.mean(scaled, axis=-1, keepdims=True)
    mean_second = jnp.mean(scaled * normed, axis=-1, keepdims=True)
    result = inverse * (scaled - mean_first - normed * mean_second)
    return (result, jnp.sum(grad_rows * normed, axis=0), jnp.sum(grad_rows, axis=0))


def after(array, *others):
    return lax.optimization_barrier((array,) + others)[0] if others else array


def take(array, start, size, axis):
    return lax.dynamic_slice_in_dim(array, start, size, axis)


kernel_params = pltpu.CompilerParams(vmem_limit_bytes=40 * 1024 * 1024)


def product(left, right, left_axis, right_axis):
    dims = (((left_axis,), (right_axis,)), ((), ()))
    return lax.dot_general(left, right, dims, preferred_element_type=wide)


def call(kernel, flops, out_shape, **settings):
    return pl.pallas_call(
        kernel,
        out_shape=out_shape,
        compiler_params=kernel_params,
        cost_estimate=pl.CostEstimate(
            flops=flops // COST_SCALE, bytes_accessed=0, transcendentals=0
        ),
        **settings,
    )


def masked_probs(query, key, valid):
    scores = jnp.where(valid, product(query, key, 1, 1), neg_large)
    expo = jnp.exp((scores - jnp.max(scores, axis=-1, keepdims=True)) * HD ** (-0.5))
    return expo * (1.0 / jnp.sum(expo, axis=-1, keepdims=True))


def valid_keys(length, shift, rows):
    token = lax.broadcasted_iota(jnp.int32, (rows, rows), 1) + shift
    return jnp.where(token < rows, token, token - rows) < length


def attend_kernel(lengths, query, key, value, context):
    rows, features = query.shape
    valid = valid_keys(lengths[pl.program_id(0)], lengths[pl.num_programs(0)], rows)
    for head in range(features // HD):
        at = slice(head * HD, (head + 1) * HD)
        probs = masked_probs(query[:, at], key[:, at], valid)
        context[:, at] = product(probs.astype(low), value[:, at], 1, 0).astype(low)


def attend_back_kernel(lengths, query, key, value, grad, grads):
    rows, features = query.shape
    valid = valid_keys(lengths[pl.program_id(0)], lengths[pl.num_programs(0)], rows)
    for head in range(features // HD):
        at, key_at, value_at = (
            slice(c * features + head * HD, c * features + (head + 1) * HD) for c in range(3)
        )
        probs = masked_probs(query[:, at], key[:, at], valid)
        grads[:, value_at] = product(probs.astype(low), grad[:, at], 0, 0).astype(low)
        prob_grad = product(grad[:, at], value[:, at], 1, 1)
        mean = jnp.sum(prob_grad * probs, axis=-1, keepdims=True)
        score_grad = (probs * (prob_grad - mean)).astype(low)
        grads[:, at] = (product(score_grad, key[:, at], 1, 0) * HD ** (-0.5)).astype(low)
        grads[:, key_at] = (product(score_grad, query[:, at], 0, 0) * HD ** (-0.5)).astype(low)


def by_sequence(kernel, flops, seq_len, lengths, projected, *arrays):
    rows, columns = projected.shape
    features = columns // 3

    def spec(width, block):
        return pl.BlockSpec((seq_len, width), lambda sequence, lengths: (sequence, block))

    size = columns if arrays else features
    return call(
        kernel,
        flops,
        jax.ShapeDtypeStruct((rows, size), low),
        grid_spec=pltpu.PrefetchScalarGridSpec(
            num_scalar_prefetch=1,
            grid=(rows // seq_len,),
            in_specs=[spec(features, c) for c in range(3)] + [spec(features, 0) for a in arrays],
            out_specs=spec(size, 0),
        ),
    )(lengths, projected, projected, projected, *arrays)


def matmul_kernel(right_axis, left, right, *rest):
    total = product(left[...], right[...], 1, right_axis)
    if len(rest) == 2:
        total = total + rest[0][...]
    rest[-1][...] = total.astype(low)


def right_spec(depth, tile, right_axis, start):
    if right_axis:
        return pl.BlockSpec((tile, depth), lambda j: (j, start // depth))
    return pl.BlockSpec((depth, tile), lambda j: (0, start // tile + j))


def column_spec(rows, tile):
    return pl.BlockSpec((rows, tile), lambda j: (0, j))


def matmul(left, right, right_axis, size, start=0, bias=None):
    rows, depth = left.shape
    tile = math.gcd(size, 512 if right_axis or start % 512 == 0 else 256)
    in_specs = [
        pl.BlockSpec((rows, depth), lambda j: (0, 0)),
        right_spec(depth, tile, right_axis, start),
    ]
    operands = [left, right]
    if bias is not None:
        in_specs.append(column_spec(1, tile))
        operands.append(bias[None])
    return call(
        functools.partial(matmul_kernel, right_axis),
        2 * rows * depth * size,
        jax.ShapeDtypeStruct((rows, size), low),
        grid=(size // tile,),
        in_specs=in_specs,
        out_specs=column_spec(rows, tile),
    )(*operands)


def gelu_tanh(values):
    return jnp.tanh((2.0 / math.pi) ** 0.5 * (values + 0.044715 * values * values * values))


def gelu_slope(values):
    tanh = gelu_tanh(values)
    inner = (2.0 / math.pi) ** 0.5 * (1.0 + 3.0 * 0.044715 * values * values)
    return 0.5 * (1.0 + tanh) + 0.5 * values * (1.0 - tanh * tanh) * inner


def up_kernel(rows, weight, bias, pre_act, hidden):
    values = product(rows[...], weight[...], 1, 0) + bias[...]
    pre_act[...] = values
    hidden[...] = (0.5 * values * (1.0 + gelu_tanh(values))).astype(low)


def up_matmul(rows, weight, bias, tile=256):
    count, units = rows.shape[0], bias.shape[0]
    return call(
        up_kernel,
        2 * rows.size * units,
        [
            jax.ShapeDtypeStruct((count, units), wide),
            jax.ShapeDtypeStruct((count, units), low),
        ],
        grid=(units // tile,),
        in_specs=[
            pl.BlockSpec(rows.shape, lambda j: (0, 0)),
            right_spec(rows.shape[1], tile, 0, 0),
            column_spec(1, tile),
        ],
        out_specs=[column_spec(count, tile)] * 2,
    )(rows, weight, bias[None])


def up_back_kernel(grads, weight, slope, pre_grad, bias_grad):
    values = product(grads[...], weight[...], 1, 0) * slope[...].astype(wide)
    rounded = values.astype(low)
    pre_grad[...] = rounded
    bias_grad[...] = jnp.sum(rounded.astype(wide), axis=0, keepdims=True)


def up_back_matmul(grads, weight, slope, tile=256):
    count, units = slope.shape
    return call(
        up_back_kernel,
        2 * grads.size * units,
        [jax.ShapeDtypeStruct((count, units), low), jax.ShapeDtypeStruct((1, units), wide)],
        grid=(units // tile,),
        in_specs=[
            pl.BlockSpec(grads.shape, lambda j: (0, 0)),
            right_spec(grads.shape[1], tile, 0, weight.shape[1] - units),
            column_spec(count, tile),
        ],
        out_specs=[column_spec(count, tile), column_spec(1, tile)],
    )(grads, weight, slope)


def pair_kernel(left_one, right_one, left_two, right_two, total):
    one = product(left_one[...], right_one[...], 0, 0)
    total[...] = (one + product(left_two[...], right_two[...], 0, 0)).astype(low)


def pair_matmul(lefts, rights, tile=256):
    rows, depth = lefts[0].shape
    columns = rights[0].shape[1]
    specs = [column_spec(rows, tile), pl.BlockSpec((rows, columns), lambda j: (0, 0))]
    return call(
        pair_kernel,
        4 * rows * depth * columns,
        jax.ShapeDtypeStruct((depth, columns), low),
        grid=(depth // tile,),
        in_specs=specs * 2,
        out_specs=pl.BlockSpec((tile, columns), lambda j: (j, 0)),
    )(lefts[0], rights[0], lefts[1], rights[1])


def local(
    inputs,
    out_grad,
    lengths,
    dealing,
    qkv_weight,
    qv_bias,
    out_weight,
    out_bias,
    attn_gain,
    attn_shift,
    up_weight,
    up_bias,
    down_weight,
    down_bias,
    ffn_gain,
    ffn_shift,
):
    groups = lax.axis_size("dp")
    ring_size = groups // 4
    index = lax.axis_index("dp")
    core, side, ring = index % 2, (index // 2) % 2, index // 4
    lane = lax.axis_index("tensor")
    core_pairs = [(i, i ^ 1) for i in range(groups)]
    side_pairs = [(i, i ^ 2) for i in range(groups)]
    ring_groups = [[4 * r + offset for r in range(ring_size)] for offset in range(4)]

    def core_swap(array):
        return lax.ppermute(array, "dp", core_pairs)

    def side_swap(array):
        return lax.ppermute(array, "dp", side_pairs)

    def ring_send(array, steps):
        return lax.ppermute(array, "dp", [(i, (i + 4 * steps) % groups) for i in range(groups)])

    def lane_swap(array):
        return lax.ppermute(array, "tensor", [(0, 1), (1, 0)])

    def in_order(bit, mine, theirs, axis):
        first = jnp.where(bit == 0, mine, theirs)
        second = jnp.where(bit == 0, theirs, mine)
        return jnp.concatenate([first, second], axis=axis)

    def parts(array, bit, axis):
        size = array.shape[axis] // 2
        return take(array, bit * size, size, axis), take(array, (1 - bit) * size, size, axis)

    seq_len, half = inputs.shape
    width = 2 * half
    per_peer = seq_len // groups
    shard = width // groups
    token_half = seq_len // 2
    features = half // 4
    units = up_weight.shape[1] // 4

    def split_weight(weight):
        mine, sent = parts(weight, core, 2)
        weight = in_order(core, mine, core_swap(sent), 0)
        mine, sent = parts(weight, side, 2)
        weight = in_order(side, mine, side_swap(sent), 0)
        return weight.reshape(4 * shard, -1)

    def split_direct(weight):
        def quarter_of(c, s):
            size = weight.shape[2] // 4
            return take(weight, (2 * c + s) * size, size, 2)

        mine = quarter_of(core, side)
        by_core = core_swap(quarter_of(1 - core, side))
        by_side = side_swap(quarter_of(core, 1 - side))
        by_both = lax.ppermute(
            quarter_of(1 - core, 1 - side), "dp", [(i, i ^ 3) for i in range(groups)]
        )
        own_side = in_order(core, mine, by_core, 0)
        return in_order(side, own_side, in_order(core, by_side, by_both, 0), 0).reshape(
            4 * shard, -1
        )

    def gather_weight(piece):
        return lax.all_gather(piece, "dp", axis=0, axis_index_groups=ring_groups, tiled=True)

    first_weights = jnp.concatenate([qkv_weight, out_weight.T[None]], axis=0).swapaxes(0, 1)
    first_piece = split_direct(first_weights)
    first_full = gather_weight(first_piece)

    small = jnp.concatenate(
        [
            v.reshape(-1)
            for v in (
                qv_bias,
                up_bias,
                out_bias,
                attn_gain,
                attn_shift,
                down_bias,
                ffn_gain,
                ffn_shift,
            )
        ]
    )[None]
    small = in_order(core, small, core_swap(after(small, first_piece)), 0)
    small = in_order(side, small, side_swap(small), 0)
    small_all = lax.dynamic_update_slice_in_dim(
        jnp.zeros((groups, small.shape[1]), low), small, ring * 4, 0
    )
    for step in range(1, ring_size):
        place = ((ring - step) % ring_size) * 4
        small_all = lax.dynamic_update_slice_in_dim(small_all, ring_send(small, step), place, 0)

    local_rows = inputs.reshape(groups, per_peer, half).swapaxes(0, 1)
    sending = jnp.take(local_rows, dealing, axis=1)
    arrived = lax.all_to_all(sending, "dp", split_axis=1, concat_axis=1, tiled=True)
    tokens = after(arrived, first_piece).reshape(seq_len, half)
    second_weights = after(up_weight, arrived), after(down_weight, arrived).T
    second_piece = split_direct(jnp.stack(second_weights, axis=1))
    second_full = gather_weight(second_piece)
    early, late = tokens[:token_half], tokens[token_half:]
    early = in_order(lane, early, lane_swap(early), 1)
    early = jnp.stack([early, side_swap(early)])
    late = jnp.stack([late, side_swap(late)])
    late = in_order(lane, late, lane_swap(late), 2)
    own_rows = jnp.stack([jnp.where(lane == 0, early, late), jnp.where(lane == 0, late, early)], 1)
    own_rows = after(own_rows.reshape(2 * seq_len, width), second_piece, small_all)
    all_rows = (own_rows, core_swap(own_rows))
    residual = own_rows[:token_half]
    grad_keep, grad_send = parts(out_grad, lane, 0)
    cotangent = in_order(lane, grad_keep, lane_swap(grad_send), 1)

    cut_one = qv_bias.size
    cut_two = cut_one + up_bias.size
    qv_full = (
        small_all[:, :cut_one]
        .reshape((groups,) + qv_bias.shape)
        .transpose(1, 2, 0, 3)
        .reshape(2, half)
    )
    up_bias_full = (
        small_all[:, cut_one:cut_two]
        .reshape((groups,) + up_bias.shape)
        .transpose(1, 0, 2)
        .reshape(-1)
    )
    vectors = (
        small_all[:, cut_two:].reshape(groups, 6, shard).transpose(1, 0, 2).reshape(6, width)
    ).astype(wide)
    out_bias_full, gain_one, shift_one, down_bias_full, gain_two, shift_two = vectors
    place = core * 2 + side
    qv_rows = take(qv_full, place * features, features, 1)
    up_bias_mine = take(up_bias_full, place * units, units, 0)

    def core_parts(left, right, start=0):
        theirs = core_swap(matmul(left[1], right, 1, width, start))
        mine = matmul(left[0], right, 1, width, start)
        return mine, theirs

    def added(both, pick):
        mine, theirs = (pick(array.reshape(2, 2, token_half, width)) for array in both)
        return mine.astype(wide) + theirs.astype(wide)

    def group_sum(both, beside_one=(), beside_two=()):
        one = side_swap(added(both, lambda a: a[1, ..., :half]).astype(low))
        two = lane_swap(added(both, lambda a: a[:, 1, :, half:]).astype(low))
        one = added(both, lambda a: a[0, ..., :half]) + after(one, *beside_one).astype(wide)
        two = added(both, lambda a: a[:, 0, :, half:]) + after(two, *beside_one).astype(wide)
        one = one[0] + after(lane_swap(one[1].astype(low)), *beside_two).astype(wide)
        two = two[0] + after(side_swap(two[1].astype(low)), *beside_two).astype(wide)
        return jnp.concatenate([one, two], axis=1)

    def group_gather(rows, beside_own=()):
        one, two = rows[:, :half], rows[:, half:]
        one = jnp.stack([one, lane_swap(one)])
        two = jnp.stack([two, side_swap(two)])
        one = jnp.stack([one, side_swap(one)])
        two = jnp.stack([two, lane_swap(two)], axis=1)
        own = jnp.concatenate([one, two], axis=3).reshape(2 * seq_len, width)
        own = after(own, *beside_own)
        return own, core_swap(own)

    sequences = jnp.stack([index, index ^ 2, index ^ 1, index ^ 3])
    group_lengths = jnp.take(lengths, jnp.take(dealing, sequences)).reshape(2, 2)
    group_lengths = jnp.concatenate(
        [group_lengths, jnp.full((2, 1), lane * token_half, jnp.int32)], axis=1
    )
    qkv_bias = jnp.concatenate([qv_rows[0], jnp.zeros_like(qv_rows[0]), qv_rows[1]]).astype(wide)
    flops = 4 * 2 * seq_len * seq_len * features
    projected, context = [], []
    for i in range(2):
        rows = after(all_rows[i], *context)
        projected.append(matmul(rows, first_full, 0, 3 * features, bias=qkv_bias))
        context.append(
            by_sequence(attend_kernel, 4 * flops, seq_len, group_lengths[i], projected[i])
        )
    attended = group_sum(core_parts(context, first_full, 3 * features)) + out_bias_full
    first, normed_one, inverse_one = norm_forward(
        residual.astype(wide) + attended, gain_one, shift_one
    )
    first_low = group_gather(first.astype(low), [second_full])

    pre_act, hidden = [], []
    for i in range(2):
        values, outs = up_matmul(after(first_low[i], *hidden), second_full, up_bias_mine.astype(wide))
        pre_act.append(values)
        hidden.append(outs)
    mixed_parts = core_parts(hidden, second_full, units)
    slope = [gelu_slope(after(values, *mixed_parts)).astype(low) for values in pre_act]
    mixed = group_sum(mixed_parts, slope) + down_bias_full
    final, normed_two, inverse_two = norm_forward(first + mixed, gain_two, shift_two)
    second_grad, gain_two_grad, shift_two_grad = norm_backward(
        cotangent.astype(wide), normed_two, inverse_two, gain_two
    )
    mixed_low = second_grad.astype(low)
    down_bias_grad = jnp.sum(mixed_low, axis=0, dtype=wide)
    mixed_grad = group_gather(mixed_low)

    def scatter(partial):
        return lax.psum_scatter(
            partial, "dp", scatter_dimension=0, axis_index_groups=ring_groups, tiled=True
        )

    def side_send(total, kinds):
        total = total.reshape(4 * shard, kinds, -1)
        mine, sent = parts(total, side, 0)
        return mine, side_swap(sent)

    def side_join(mine, theirs):
        return in_order(side, mine, theirs, 2)

    def core_join(total):
        mine, sent = parts(total, core, 0)
        return in_order(core, mine, core_swap(sent), 2).astype(wide)

    pre_grad = [up_back_matmul(mixed_grad[0], second_full, slope[0])]
    mixed_grad = (mixed_grad[0], after(mixed_grad[1], pre_grad[0][0]))
    down_partial = pair_matmul(mixed_grad, hidden)
    down_sum = scatter(down_partial)
    pre_grad.append(up_back_matmul(after(mixed_grad[1], down_partial), second_full, slope[1]))
    pre_grad, up_bias_grad = zip(*pre_grad, strict=True)
    both = core_parts(pre_grad, second_full)
    up_partial = pair_matmul(first_low, [after(grads, *both) for grads in pre_grad])
    up_sum = scatter(up_partial)
    first_grad = second_grad + group_sum(both, [up_partial], [down_sum])
    attn_total_grad, gain_one_grad, shift_one_grad = norm_backward(
        first_grad, normed_one, inverse_one, gain_one
    )
    attended_low = attn_total_grad.astype(low)
    out_bias_grad = jnp.sum(attended_low, axis=0, dtype=wide)
    attended_grad = group_gather(attended_low)
    down_sum = side_send(down_sum, 1)
    stacked, parts_grad = [], []
    for i in range(2):
        rows = after(attended_grad[i], *parts_grad)
        if i:
            rows = after(rows, down_sum[1])
        context_grad = matmul(rows, first_full, 0, features, 3 * features)
        stacked.append(
            by_sequence(
                attend_back_kernel,
                8 * flops,
                seq_len,
                group_lengths[i],
                projected[i],
                context_grad,
            )
        )
        parts_grad.append(matmul(stacked[i], first_full, 1, width))
    mine, theirs = parts_grad
    qkv_partial = pair_matmul(all_rows, [after(grads, theirs) for grads in stacked])
    qkv_sum = scatter(qkv_partial)
    theirs = core_swap(theirs)
    theirs = after(theirs, up_sum)

    quarter = half // 2
    both = tuple(array.reshape(2, seq_len, width) for array in (after(mine, up_sum[1]), theirs))

    def summed(pick):
        return sum(pick(array).astype(wide) for array in both)

    def across(array):
        return jnp.concatenate([array[..., :quarter], array[..., half : half + quarter]], axis=-1)

    def of_lane(bit):
        return lambda array: take(array, bit * half + quarter, quarter, 2)

    def lane_swap_rows(array):
        array = lane_swap(array)
        return jnp.concatenate([array[..., token_half:, :], array[..., :token_half, :]], axis=-2)

    one_sent = summed(lambda array: across(array[1])).astype(low)
    two_sent = summed(of_lane(1 - lane)).astype(low)
    one, two = side_swap(one_sent), lane_swap_rows(two_sent)
    out_partial = pair_matmul(attended_grad, [after(rows, one_sent, two_sent) for rows in context])
    out_sum = scatter(out_partial)
    one = summed(lambda array: across(array[0])) + one.astype(wide)
    two = summed(of_lane(lane)) + two.astype(wide)
    one_sent = take(one, (1 - lane) * quarter, quarter, 1).astype(low)
    two_sent = two[1].astype(low)
    down_weight_grad = core_join(after(side_join(*down_sum), one_sent))[:, 0].T
    one_theirs = after(lane_swap(one_sent), down_weight_grad, out_partial)
    one_theirs = jnp.concatenate([one_theirs[token_half:], one_theirs[:token_half]], axis=0)
    one = take(one, lane * quarter, quarter, 1) + one_theirs.astype(wide)
    two = two[0] + side_swap(two_sent).astype(wide)
    own_attended = take(attended_grad[0][:seq_len], lane * half, half, 1)
    in_half = (jnp.concatenate([one, two], axis=1) + own_attended.astype(wide)).astype(low)
    in_half = in_order(lane, in_half[:token_half], in_half[token_half:], 0)
    back_rows = after(in_half, qkv_sum).reshape(per_peer, groups, half)
    out_keep, out_send = parts(final.astype(low), lane, 1)
    outputs = in_order(lane, out_keep, lane_swap(after(out_send, qkv_sum)), 0)
    qkv_bias_sum = sum(jnp.sum(after(s, two_sent), axis=0, dtype=wide) for s in stacked)
    qkv_bias_sum = qkv_bias_sum.reshape(3, features)
    qv_grad = jnp.stack([qkv_bias_sum[0], qkv_bias_sum[2]])
    def spread(mine, size):
        full = jnp.zeros(mine.shape[:-1] + (4 * size,), wide)
        return lax.dynamic_update_slice_in_dim(full, mine, place * size, mine.ndim - 1)

    qv_spread = (
        spread(qv_grad, features)
        .reshape(2, qv_bias.shape[1], groups, qv_bias.shape[2])
        .transpose(2, 0, 1, 3)
        .reshape(groups, -1)
    )
    up_spread = (
        spread((up_bias_grad[0] + up_bias_grad[1])[0], units)
        .reshape(up_bias.shape[0], groups, up_bias.shape[1])
        .transpose(1, 0, 2)
        .reshape(groups, -1)
    )
    vector_spread = (
        jnp.stack(
            [
                out_bias_grad,
                gain_one_grad,
                shift_one_grad,
                down_bias_grad,
                gain_two_grad,
                shift_two_grad,
            ]
        )
        .reshape(6, groups, shard)
        .transpose(1, 0, 2)
        .reshape(groups, -1)
    )
    packed = jnp.concatenate([qv_spread, up_spread, vector_spread], axis=1)
    packed = after(packed, qkv_sum)

    up_weight_grad = core_join(side_join(*side_send(after(up_sum, two_sent), 1)))[:, 0]
    returned = lax.all_to_all(back_rows, "dp", split_axis=1, concat_axis=1, tiled=True)
    inverse_order = (
        jnp.zeros((groups,), jnp.int32).at[dealing].set(jnp.arange(groups, dtype=jnp.int32))
    )
    in_grad = jnp.take(returned, inverse_order, axis=1).swapaxes(0, 1).reshape(seq_len, half)

    out_weight_grad = core_join(side_join(*side_send(after(out_sum, qkv_sum), 1)))[:, 0].T
    qkv_grad = core_join(side_join(*side_send(qkv_sum, 3))).swapaxes(0, 1)

    packed = packed.reshape(ring_size, 2, 2, packed.shape[1])
    mine, sent = parts(packed, core, 2)
    packed = (mine + core_swap(sent))[:, :, 0]
    mine, sent = parts(packed, side, 1)
    packed = (mine + side_swap(sent))[:, 0]
    small_sum = take(packed, ring, 1, 0)
    for step in range(1, ring_size):
        sent = take(packed, (ring + step) % ring_size, 1, 0)
        small_sum = small_sum + ring_send(sent, step)
    small_sum = small_sum[0]
    vector_sum = small_sum[cut_two:]
    vector_sum = (vector_sum + lane_swap(vector_sum)).reshape(6, shard)
    return (
        outputs,
        in_grad,
        qkv_grad,
        small_sum[:cut_one].reshape(qv_bias.shape),
        out_weight_grad,
        vector_sum[0],
        vector_sum[1],
        vector_sum[2],
        up_weight_grad,
        small_sum[cut_one:cut_two].reshape(up_bias.shape),
        down_weight_grad,
        vector_sum[3],
        vector_sum[4],
        vector_sum[5],
    )


def solution(mesh):
    placed = (
        P("dp", "tensor"),
        P("dp", "tensor"),
        P(),
        P(),
        P(None, "dp", "tensor"),
        P(None, "tensor", "dp"),
        P("tensor", "dp"),
        P("dp"),
        P("dp"),
        P("dp"),
        P("dp", "tensor"),
        P("tensor", "dp"),
        P("tensor", "dp"),
        P("dp"),
        P("dp"),
        P("dp"),
    )
    return jax.shard_map(
        local,
        mesh=mesh,
        in_specs=placed,
        out_specs=(
            P("dp", "tensor"),
            P("dp", "tensor"),
            P(None, "dp", "tensor"),
            P(None, "tensor", "dp"),
            P("tensor", "dp"),
            P("dp"),
            P("dp"),
            P("dp"),
            P("dp", "tensor"),
            P("tensor", "dp"),
            P("tensor", "dp"),
            P("dp"),
            P("dp"),
            P("dp"),
        ),
        check_vma=False,
    )
```
